32 devices in a mesh: pole: 4 (over y, x), sub: 8 (over z, core).
Axes of the slice: x: 2, y: 2, z: 4, core: 2. Of those that a mesh axis runs over, the one named last changes fastest.
Arguments:
- start_block: float32 [32768, 128], P('sub'), may hold values from -400 to 400
- inverses: float32 [4, 64, 512, 512], P('pole', 'sub'), may hold values from -1 to 3
- iface_rows: int32 [64, 2, 128], P('sub'), may hold values from 0 to 511, as said below
- neighbors: int32 [64, 2], P('sub'), may hold values from 0 to 63, as said below
- couplings: float32 [64, 2, 128], P('sub'), may hold values from 0.25 to 1
- pole_weights: float32 [4], P('pole'), may hold values from 0.25 to 1
Outputs:
- ortho_basis: float32 [32768, 128], P(('sub', 'pole'))
The draws below stay inside these ranges and needn't reach their ends.
Inputs may be any that keep to these rules, and one draw needn't show every extreme that they name: `iface_rows`: in each subdomain the 256 listed rows are distinct. Subdomain j lies on index j // 8 of sub. neighbors[j, 0] lies on the previous index and neighbors[j, 1] on the next one, cyclically; over the subdomains of one index, the values in column 0 are the previous index's 8 subdomains, each once, and those in column 1 the next index's, each once.
All inputs are finite; a program needn't handle non-finite values.
Results may differ from the reference program's by a relative error of at most 0.0002.
Values sent between devices are 32-bit elements; how exact they have to be, the bound alone decides.
No kernel may reach another device: no remote copies, remote signals or barrier semaphores. Data moves between devices by JAX's collectives and lax.ppermute only.
A program may use at most 64 MiB of HBM per device.

```python
import math
import jax
import jax.numpy as jnp
from jax import lax

BLOCK = 512
VECS = 128
IFACE = 128
SUB_DEV = 8
SUBS = 64
NROWS = 32768
POLES = 4


def draw_start_block(key, part):
    noise_key, row_key, col_key = jax.random.split(key, 3)
    position = jnp.arange(NROWS, dtype=jnp.float32) / NROWS
    entries = jax.random.truncated_normal(noise_key, -4.0, 4.0, (NROWS, VECS), jnp.float32)
    row_scale = jnp.exp(jax.random.uniform(row_key, (NROWS, 1), jnp.float32, 0.0, math.log(10.0)))
    row_scale = row_scale * (1.0 + 2.0 * position)[:, None]
    col_scale = jnp.exp(jax.random.uniform(col_key, (1, VECS), jnp.float32, 0.0, math.log(10.0)))
    return 0.1 * entries * row_scale * col_scale


def draw_inverses(key, part):
    noise_key, diag_key = jax.random.split(key, 2)
    full_shape = (POLES, SUBS, BLOCK, BLOCK)
    spread = 0.4 * jax.random.truncated_normal(noise_key, -4.0, 4.0, full_shape, jnp.float32) / math.sqrt(BLOCK)
    diagonal = jax.random.uniform(diag_key, (POLES, SUBS, 1, BLOCK), jnp.float32, 0.5, 1.5)
    return spread + jnp.eye(BLOCK, dtype=jnp.float32) * diagonal


def draw_iface_rows(key, part):
    keys = jax.random.split(jax.random.fold_in(key, 21), SUBS)
    orders = jax.vmap(lambda single: jax.random.permutation(single, BLOCK))(keys)
    return orders[:, :2 * IFACE].reshape(SUBS, 2, IFACE).astype(jnp.int32)


def draw_neighbors(key, part):
    groups = SUBS // SUB_DEV
    low_keys = jax.random.split(jax.random.fold_in(key, 31), groups)
    high_keys = jax.random.split(jax.random.fold_in(key, 32), groups)
    low_order = jax.vmap(lambda single: jax.random.permutation(single, SUB_DEV))(low_keys)
    high_order = jax.vmap(lambda single: jax.random.permutation(single, SUB_DEV))(high_keys)
    device_ids = jnp.arange(groups, dtype=jnp.int32)[:, None]
    before = (device_ids - 1) % groups * SUB_DEV + low_order
    following = (device_ids + 1) % groups * SUB_DEV + high_order
    return jnp.stack([before.reshape(-1), following.reshape(-1)], axis=1).astype(jnp.int32)


def steps_of(stream_key, shape, cuts, low, top_value):
    gain = 1.0
    for dim, blocks in cuts:
        heights = jax.random.uniform(jax.random.fold_in(jax.random.fold_in(stream_key, 6), dim), (blocks,), jnp.float32, low / len(cuts), top_value / len(cuts))
        gain = gain * jnp.repeat(jnp.exp(heights), shape[dim] // blocks).reshape((-1,) + (1,) * (len(shape) - 1 - dim))
    return gain


def setup_inputs(seed: int = 0) -> dict:
    arg_keys = jax.random.split(jax.random.key(seed), 7)
    start_block = draw_start_block(jax.random.fold_in(arg_keys[6], 71), 0)
    inverses = draw_inverses(jax.random.fold_in(arg_keys[6], 71), 0)
    iface_rows = draw_iface_rows(jax.random.fold_in(arg_keys[6], 71), 0)
    neighbors = draw_neighbors(jax.random.fold_in(arg_keys[6], 71), 0)
    couplings = jnp.clip(jnp.exp(math.log(1.0) - 1.3862944 * jax.random.uniform(arg_keys[4], (SUBS, 2, IFACE), jnp.float32) ** steps_of(arg_keys[4], (SUBS, 2, IFACE), ((0, 8),), -0.2, 0.2)), 0.25, 1.0)
    pole_weights = jnp.clip(0.25 + 0.75 * jax.random.uniform(arg_keys[5], (POLES,), jnp.float32) ** steps_of(arg_keys[5], (POLES,), ((0, 4),), -0.2, 0.2), 0.25, 1.0)
    return {"start_block": start_block, "inverses": inverses, "iface_rows": iface_rows, "neighbors": neighbors, "couplings": couplings, "pole_weights": pole_weights}


precise = lax.Precision.HIGHEST

def apply_blocks(blocks, fields):
    return jnp.einsum('sij,sjv->siv', blocks.astype(jnp.float32), fields.astype(jnp.float32), precision=precise, preferred_element_type=jnp.float32)

def add_coupled(fields, iface_rows, neighbor_vals, couplings):

    def one_sub(field_one, rows_one, terms_one):
        field_one = field_one.at[rows_one[0]].add(terms_one[0])
        return field_one.at[rows_one[1]].add(terms_one[1])
    return jax.vmap(one_sub)(fields, iface_rows, couplings[..., None] * neighbor_vals)

def reference(start_block, inverses, iface_rows, neighbors, couplings, pole_weights):
    fields = start_block.reshape(SUBS, BLOCK, VECS)
    offsets = (jnp.arange(SUBS, dtype=jnp.int32) * BLOCK)[:, None, None]
    flat_index = (iface_rows + offsets).reshape(-1).astype(jnp.int32)

    def one_pole(summed_poles, pole_in):
        blocks, weight = pole_in
        first_pass = apply_blocks(blocks, fields)
        side_rows = jnp.take(first_pass.reshape(NROWS, VECS), flat_index, axis=0).reshape(SUBS, 2, IFACE, VECS)
        low_terms = side_rows[neighbors[:, 0], 1]
        high_terms = side_rows[neighbors[:, 1], 0]
        corrected = add_coupled(fields, iface_rows, jnp.stack([low_terms, high_terms], 1), couplings)
        return (summed_poles + weight * apply_blocks(blocks, corrected), None)
    summed_poles, leftover = lax.scan(one_pole, jnp.zeros((SUBS, BLOCK, VECS), jnp.float32), (inverses, pole_weights))
    filtered = summed_poles.reshape(NROWS, VECS)
    gram_matrix = jnp.dot(filtered.T.astype(jnp.float32), filtered.astype(jnp.float32), precision=precise, preferred_element_type=jnp.float32)
    lower_factor = jnp.linalg.cholesky(gram_matrix)
    solved = lax.linalg.triangular_solve(lower_factor, filtered, left_side=False, lower=True, transpose_a=True)
    return math.sqrt(NROWS) * solved
```

```python
import functools
import math

import jax
import jax.numpy as jnp
from jax import lax
from jax.experimental import pallas as pl
from jax.experimental.pallas import tpu as pltpu
from jax.sharding import PartitionSpec as P

f32 = jnp.float32
bf16 = jnp.bfloat16


def split(x):
    high = x.astype(bf16)
    low = (x - high.astype(f32)).astype(bf16)
    return high, low


def mm(a, b):
    return jnp.dot(a, b, preferred_element_type=f32)


def split_dot(a, b):
    width = b.shape[1]
    both = jnp.concatenate(split(b), axis=1)
    both = mm(a[0], both) + mm(a[1], both)
    return both[:, :width] + both[:, width:]


def turn(x):
    return pltpu.roll(x, x.shape[1] // 2, 1)


def left_lanes(x):
    return lax.broadcasted_iota(jnp.int32, x.shape, 1) < x.shape[1] // 2


def pack(top, bottom, half):
    if half == 0:
        return jnp.where(left_lanes(top), top, turn(bottom))
    return jnp.where(left_lanes(top), turn(top), bottom)


def sub_parity():
    return lax.rem(lax.axis_index("sub"), 2)


def pack_side(side_ref, s, half):
    rows = side_ref.shape[1] // 2
    return pack(side_ref[s, :rows, :], side_ref[s, rows:, :], half)


def gather_side(s, side, pass_ref, rows, side_ref, out_ref):
    for k in range(rows.shape[2]):
        side_ref[s, k : k + 1, :] = pass_ref[s, pl.ds(rows[s, side, k], 1), :]
    out_ref[s] = pack_side(side_ref, s, 0)


def first_kernel(weight, inv_hbm, field_hbm, rows_hbm, pass_ref, side_ref, off_ref,
                 inv_buf, field_buf, rows, inv_sems, field_sems, rows_sem):
    count = field_buf.shape[0]
    rows_copy = pltpu.make_async_copy(rows_hbm, rows, rows_sem)
    rows_copy.start()

    def copies(s):
        return (
            pltpu.make_async_copy(field_hbm.at[s], field_buf.at[s], field_sems.at[s]),
            pltpu.make_async_copy(inv_hbm.at[s], inv_buf.at[s], inv_sems.at[s]),
        )

    for s in range(count):
        for copy in copies(s):
            copy.start()
    rows_copy.wait()
    parity = sub_parity()

    def one_sub(s, carry):
        for copy in copies(s):
            copy.wait()
        gather_side(jnp.maximum(s - 1, 0), parity, pass_ref, rows, side_ref, off_ref)
        pass_ref[s] = weight[0] * split_dot(split(inv_buf[s]), field_buf[s])
        return carry

    lax.fori_loop(0, count, one_sub, 0)
    gather_side(count - 1, parity, pass_ref, rows, side_ref, off_ref)


def columns_kernel(inv_hbm, rows_hbm, rows_ref, coup_ref, near_ref, pass_ref, off_side_ref,
                   high_cols_ref, low_cols_ref, pass0_ref, pass1_ref, off_ref, on0_ref, on1_ref, table_ref,
                   inv_buf, on_side_ref, rows, inv_sems, rows_sem):
    count, block_len = inv_buf.shape[:2]
    iface_len = rows_ref.shape[2]
    quarter = block_len // 4

    def copy(s):
        return pltpu.make_async_copy(inv_hbm.at[s], inv_buf.at[s], inv_sems.at[s])

    rows_copy = pltpu.make_async_copy(rows_hbm, rows, rows_sem)
    rows_copy.start()
    for s in range(count):
        copy(s).start()
    parity = sub_parity()
    for spot, side in enumerate((parity, 1 - parity)):
        near = lax.rem(near_ref[pl.ds(side, 1), :], count)
        for s in range(count):
            table_ref[spot, s] = jnp.broadcast_to(near[:, s : s + 1], table_ref.shape[2:])
    place = lax.broadcasted_iota(jnp.int32, (block_len, 2 * iface_len), 0)
    rows_copy.wait()

    def one_sub(s, carry):
        copy(s).wait()
        gather_side(s, 1 - parity, pass_ref, rows, on_side_ref, on0_ref)
        on1_ref[s] = pack_side(on_side_ref, s, 1)
        off_ref[s] = pack_side(off_side_ref, s, 1)
        for half, out_ref in enumerate((pass0_ref, pass1_ref)):
            for way in range(2):
                at = 2 * way * quarter
                out_ref[s, way] = pack(
                    pass_ref[s, at : at + quarter, :], pass_ref[s, at + quarter : at + 2 * quarter, :], half
                )
        at, coup = (
            jnp.concatenate([ref[s, pl.ds(side, 1), :] for side in (parity, 1 - parity)], axis=1)
            for ref in (rows_ref, coup_ref)
        )
        pick = (at == place).astype(f32).astype(bf16)
        inv_high, inv_low = split(inv_buf[s])
        high_cols_ref[s], low_cols_ref[s] = split((mm(inv_high, pick) + mm(inv_low, pick)) * coup)
        return carry

    lax.fori_loop(0, count, one_sub, 0)


def second_kernel(poles, sent, table_ref, high_ref, low_ref, pass_ref, off_ref, on_ref, out_ref):
    count, ways, quarter, _ = pass_ref.shape
    per_owner = count // poles
    steps = poles.bit_length() - 1
    me, parity = lax.axis_index("pole"), sub_parity()
    for r in range(sent, poles, 2):
        turned = sum(1 << (steps - 1 - step) for step in range(steps) if r >> step & 1)
        owner = me ^ jnp.where(parity == 0, r, turned)
        for c in range(per_owner):
            sub = owner * per_owner + c
            terms = []
            for spot, ref in enumerate((off_ref, on_ref)):
                near = jnp.concatenate([table_ref[spot, sub]] * (ref.shape[1] // 8), axis=0)
                side = ref[0]
                for at in range(1, count):
                    side = jnp.where(near == at, ref[at], side)
                turned_side = turn(side)
                terms += [
                    jnp.where(left_lanes(side), side, turned_side),
                    jnp.where(left_lanes(side), turned_side, side),
                ]
            terms = jnp.concatenate(terms, axis=0)
            high = terms.astype(bf16).astype(f32)
            both = jnp.where(left_lanes(terms), high, terms - high).astype(bf16)
            out = mm(high_ref[sub], both) + mm(low_ref[sub], both)
            out = out + turn(out)
            for way in range(ways):
                at = 2 * way * quarter
                top, bottom = out[at : at + quarter], out[at + quarter : at + 2 * quarter]
                to = (c * ways + way) * quarter
                out_ref[r // 2, to : to + quarter, :] = (
                    jnp.where(left_lanes(top), top, bottom) + pass_ref[sub, way]
                )


def gram_kernel(groups, per_owner, *refs):
    count = sum(groups)
    ins, (halves_ref, gram_ref, out_ref) = refs[:count], refs[count:]
    parts = []
    at = 0
    for size in groups:
        parts.append(functools.reduce(jnp.add, [ref[0] for ref in ins[at : at + size]]))
        at += size
    quarter = out_ref.shape[0] // (4 * per_owner)
    for way in range(2):
        for c in range(per_owner):
            first, second = (part[(2 * c + way) * quarter : (2 * c + way + 1) * quarter] for part in parts)
            at = (4 * c + 2 * way) * quarter
            out_ref[at : at + quarter, :] = jnp.where(left_lanes(first), first, turn(second))
            out_ref[at + quarter : at + 2 * quarter, :] = jnp.where(left_lanes(first), turn(first), second)
    high, low = split(out_ref[...])
    width = out_ref.shape[1]
    halves = jnp.concatenate([high, low], axis=1)
    halves_ref[...] = halves
    both = lax.dot_general(high, halves, (((0,), (0,)), ((), ())), preferred_element_type=f32)
    cross = both[:, width:]
    gram = both[:, :width] + (cross + cross.T)
    half = width // 2
    row = lax.broadcasted_iota(jnp.int32, (half, width), 0)
    col = lax.broadcasted_iota(jnp.int32, (half, width), 1)
    gram_ref[:half, :] = jnp.where(row > col - half, jnp.where(col < half, gram[half:], turn(gram[:half])), gram[half:])
    diag = jnp.sum(jnp.where(row == col, gram[:half], 0.0), axis=0, keepdims=True)
    gram_ref[half:, :] = jnp.broadcast_to(diag, (gram_ref.shape[0] - half, width))


def unpacked(gram):
    width = gram.shape[1]
    half = width // 2
    row = lax.broadcasted_iota(jnp.int32, (half, width), 0)
    col = lax.broadcasted_iota(jnp.int32, (half, width), 1)
    top = gram[:half]
    diag = jnp.broadcast_to(gram[half : half + 1], top.shape)
    first = jnp.where(row > col, turn(top), jnp.where(row == col, 0.5 * diag, 0.0))
    last = jnp.where(col < half, top, jnp.where(col - half > row, top, jnp.where(col - half == row, 0.5 * top, 0.0)))
    lower = jnp.concatenate([first, last], axis=0)
    return lower + lower.T


def four_pivots(a):
    det = a[0][0] * a[1][1] - a[1][0] * a[1][0]
    inv = 1.0 / det
    p00, p01, p11 = a[1][1] * inv, -a[1][0] * inv, a[0][0] * inv
    g20, g21 = a[2][0] * p00 + a[2][1] * p01, a[2][0] * p01 + a[2][1] * p11
    g30, g31 = a[3][0] * p00 + a[3][1] * p01, a[3][0] * p01 + a[3][1] * p11
    s22 = a[2][2] - (g20 * a[2][0] + g21 * a[2][1])
    s32 = a[3][2] - (g30 * a[2][0] + g31 * a[2][1])
    s33 = a[3][3] - (g30 * a[3][0] + g31 * a[3][1])
    inv = 1.0 / (s22 * s33 - s32 * s32)
    q00, q01, q11 = s33 * inv, -s32 * inv, s22 * inv

    def solve(r):
        z2 = r[2] - (g20 * r[0] + g21 * r[1])
        z3 = r[3] - (g30 * r[0] + g31 * r[1])
        w2, w3 = q00 * z2 + q01 * z3, q01 * z2 + q11 * z3
        w0 = p00 * r[0] + p01 * r[1] - (g20 * w2 + g30 * w3)
        w1 = p01 * r[0] + p11 * r[1] - (g21 * w2 + g31 * w3)
        return [w0, w1, w2, w3]

    def normalized(r):
        z2 = r[2] - (g20 * r[0] + g21 * r[1])
        z3 = r[3] - (g30 * r[0] + g31 * r[1])
        root0, root2 = lax.rsqrt(a[0][0]), lax.rsqrt(s22)
        l10, l32 = a[1][0] * (root0 * root0), s32 * (root2 * root2)
        return [
            r[0] * root0,
            (r[1] - l10 * r[0]) * lax.rsqrt(a[1][1] - l10 * a[1][0]),
            z2 * root2,
            (z3 - l32 * z2) * lax.rsqrt(s33 - l32 * s32),
        ]

    return solve, normalized


def combined(weights, rows):
    return (weights[0] * rows[0] + weights[1] * rows[1]) + (weights[2] * rows[2] + weights[3] * rows[3])


def inverse_rows(gram, tile_refs):
    vecs = gram.shape[0]
    tile, block = 8, 4
    tiles = vecs // tile
    sub_id = lax.broadcasted_iota(jnp.int32, (tile, vecs), 0)
    lane_id = lax.broadcasted_iota(jnp.int32, (tile, vecs), 1)
    diag = [jnp.where(lane_id == sub_id + t * tile, gram[t * tile : (t + 1) * tile], 0.0) for t in range(tiles)]
    scale = lax.rsqrt(jnp.sum(functools.reduce(jnp.add, diag), axis=0, keepdims=True))
    left, right = [], []
    for t in range(tiles):
        own = lax.rsqrt(jnp.sum(diag[t], axis=1, keepdims=True))
        left.append(gram[t * tile : (t + 1) * tile] * scale * own)
        right.append(jnp.where(lane_id == sub_id + t * tile, jnp.broadcast_to(scale, (tile, vecs)), 0.0))

    def lane(x, k):
        return jnp.broadcast_to(x[:, k : k + 1], (tile, vecs))

    def rows_of(tiles_now):
        for ref, x in zip(tile_refs, tiles_now):
            ref[...] = x
        return [[ref[pl.ds(i, tile, stride=0), :] for i in range(tile)] for ref in tile_refs]

    done = []
    for at in range(tiles):
        k = at * tile
        both_rows = rows_of((left[at], right[at]))
        a = [[lane(both_rows[0][i], k + j) for i in range(j + 1)] for j in range(tile)]
        solve, normalized = four_pivots(a)
        inner = [solve(a[j][:block]) for j in range(block, tile)]
        after = [
            [a[block + j][block + i] - combined(a[block + j], inner[i]) for i in range(j + 1)] for j in range(block)
        ]
        solve_after, normalized_after = four_pivots(after)
        weights = []
        for rows in both_rows:
            first = solve(rows[:block])
            later = [rows[block + j] - combined(a[block + j], first) for j in range(block)]
            second = solve_after(later)
            first = [w - combined([inner[j][i] for j in range(block)], second) for i, w in enumerate(first)]
            weights.append(first + second)
        done += [x[:1] for x in normalized(rows[:block]) + normalized_after(later)]
        for t in range(at + 1, tiles):
            cols = [lane(left[t], k + i) for i in range(tile)]
            for part, w in zip((left, right), weights):
                part[t] = part[t] - (combined(cols[:block], w[:block]) + combined(cols[block:], w[block:]))
    return jnp.concatenate(done, axis=0)


def ortho_kernel(scale, *refs):
    *gram_refs, halves_ref, out_ref, left_ref, right_ref = refs
    gram = functools.reduce(jnp.add, [ref[...] for ref in gram_refs])
    width = gram.shape[1]
    inverse = jnp.concatenate(split(inverse_rows(unpacked(gram), (left_ref, right_ref)) * scale), axis=0)
    both = lax.dot_general(
        halves_ref[...],
        jnp.concatenate([inverse, inverse], axis=1),
        (((1,), (1,)), ((), ())),
        preferred_element_type=f32,
    )
    out_ref[...] = both[:, :width] + both[:, width:]


def call(body, out_shape, flops=0, moved=0, limit=24, **kw):
    return pl.pallas_call(
        body,
        out_shape=out_shape,
        compiler_params=pltpu.CompilerParams(vmem_limit_bytes=limit * 1024 * 1024),
        cost_estimate=pl.CostEstimate(flops=flops, bytes_accessed=moved, transcendentals=0),
        **kw,
    )


def swap(value, even, odd):
    poles, groups = lax.axis_size("pole"), lax.axis_size("sub")
    pairs = []
    for p in range(poles):
        for s in range(groups):
            pole_mask, sub_mask = odd if s % 2 else even
            pairs.append((p * groups + s, (p ^ pole_mask) * groups + (s ^ sub_mask)))
    return lax.ppermute(value, ("pole", "sub"), pairs)


def per_device(start_block, inverses, iface_rows, neighbors, couplings, pole_weights):
    blocks = inverses[0]
    sub_count, block_len = blocks.shape[:2]
    vecs = start_block.shape[1]
    iface_len = iface_rows.shape[2]
    poles, groups = lax.axis_size("pole"), lax.axis_size("sub")
    fields = start_block.reshape(sub_count, block_len, vecs)
    shape = jax.ShapeDtypeStruct
    smem = pl.BlockSpec(memory_space=pltpu.SMEM)
    hbm = pl.BlockSpec(memory_space=pltpu.HBM)
    vmem = pl.BlockSpec(memory_space=pltpu.VMEM)
    block_bytes = sub_count * block_len * block_len * 4
    field_bytes = sub_count * block_len * vecs * 4
    packed = shape((sub_count, iface_len // 2, vecs), f32)
    in_hbm = functools.partial(pltpu.with_memory_space_constraint, memory_space=pltpu.HBM)
    in_vmem = functools.partial(pltpu.with_memory_space_constraint, memory_space=pltpu.VMEM)
    sides = shape((sub_count, iface_len, vecs), f32)
    first, off_side, off0 = call(
        first_kernel,
        (shape(fields.shape, f32), sides, packed),
        flops=8 * sub_count * block_len * block_len * vecs,
        moved=block_bytes + 3 * field_bytes,
        in_specs=[smem, hbm, hbm, hbm],
        out_specs=[vmem] * 3,
        scratch_shapes=[
            pltpu.VMEM(blocks.shape, f32),
            pltpu.VMEM(fields.shape, f32),
            pltpu.SMEM(iface_rows.shape, jnp.int32),
            pltpu.SemaphoreType.DMA((sub_count,)),
            pltpu.SemaphoreType.DMA((sub_count,)),
            pltpu.SemaphoreType.DMA,
        ],
        name="first_pass",
    )(pole_weights, in_hbm(blocks), in_hbm(fields), in_hbm(iface_rows))
    first, off_side = in_vmem(first), in_vmem(off_side)
    across = [(s, (s + (1 if s % 2 else -1)) % groups) for s in range(groups)]
    inside = [(s, s ^ 1) for s in range(groups)]
    off_in0 = lax.ppermute(off0, "sub", across)
    cols = shape((sub_count, block_len, 2 * iface_len), bf16)
    pass_half = shape((sub_count, 2, block_len // 4, vecs), f32)
    cols_high, cols_low, pass0, pass1, off1, on0, on1, table = call(
        columns_kernel,
        (cols, cols, pass_half, pass_half, packed, packed, packed, shape((2, sub_count, 8, vecs), jnp.int32)),
        flops=8 * sub_count * block_len * block_len * iface_len,
        moved=2 * block_bytes,
        in_specs=[hbm] * 2 + [vmem] * 5,
        out_specs=[vmem] * 8,
        scratch_shapes=[
            pltpu.VMEM(blocks.shape, f32),
            pltpu.VMEM(sides.shape, f32),
            pltpu.SMEM(iface_rows.shape, jnp.int32),
            pltpu.SemaphoreType.DMA((sub_count,)),
            pltpu.SemaphoreType.DMA,
        ],
        name="interface_columns",
    )(in_hbm(blocks), in_hbm(iface_rows), iface_rows, couplings, neighbors.T, first, off_side)
    on_in0 = lax.ppermute(on0, "sub", inside)
    halves = [(off_in0, on_in0), (lax.ppermute(off1, "sub", across), lax.ppermute(on1, "sub", inside))]
    cols_high, cols_low, pass0, pass1 = (in_vmem(v) for v in (cols_high, cols_low, pass0, pass1))

    per_owner = sub_count // poles
    steps = poles.bit_length() - 1
    parts = shape((poles // 2, per_owner * block_len // 2, vecs), f32)
    pending = []
    for own_pass, (off_in, on_in) in zip((pass0, pass1), halves):
        send, keep = (
            call(
                functools.partial(second_kernel, poles, sent),
                parts,
                flops=4 * sub_count * block_len * 2 * iface_len * vecs,
                moved=2 * sub_count * block_len * vecs * 4,
                in_specs=[vmem] * 6,
                out_specs=vmem,
                name="second_pass",
            )(table, cols_high, cols_low, own_pass, off_in, on_in)
            for sent in (1, 0)
        )
        pending.append((send, [keep]))

    for step in range(steps):
        masks = (1 << step, 0), (1 << (steps - 1 - step), 0)
        for half, (send, kept) in enumerate(pending):
            kept = kept + [swap(send, *masks)]
            if kept[0].shape[0] > 1:
                send = functools.reduce(jnp.add, [v[1::2] for v in kept])
                kept = [v[0::2] for v in kept]
            pending[half] = (send, kept)

    summands = [kept for _, kept in pending]
    sizes = tuple(len(kept) for kept in summands)
    own_rows = per_owner * block_len
    basis_halves, gram = call(
        functools.partial(gram_kernel, sizes, per_owner),
        (shape((own_rows, 2 * vecs), bf16), shape((vecs // 2 + 8, vecs), f32)),
        flops=4 * own_rows * vecs * vecs,
        moved=5 * own_rows * vecs * 4,
        in_specs=[vmem] * sum(sizes),
        out_specs=[vmem] * 2,
        scratch_shapes=[pltpu.VMEM((own_rows, vecs), f32)],
        name="gram",
    )(*[v for kept in summands for v in kept])

    stages = [[(0, 1)], [(r, 0) for r in range(1, poles)]]
    base = 2
    while base < groups:
        radix = min(4, groups // base)
        stages.append([(0, base * r) for r in range(1, radix)])
        base *= radix
    grams = [gram]
    for masks in stages:
        total = functools.reduce(jnp.add, grams)
        grams = [total] + [swap(total, m, m) for m in masks]

    total_rows = sub_count * block_len * groups
    return call(
        functools.partial(ortho_kernel, math.sqrt(total_rows)),
        shape((own_rows, vecs), f32),
        flops=6 * own_rows * vecs * vecs,
        moved=2 * own_rows * vecs * 4,
        in_specs=[vmem] * (len(grams) + 1),
        out_specs=vmem,
        scratch_shapes=[pltpu.VMEM((8, vecs), f32)] * 2,
        name="ortho",
    )(*grams, basis_halves)


def solution(mesh):
    placed = (
        P("sub", None),
        P("pole", "sub", None, None),
        P("sub", None, None),
        P("sub", None),
        P("sub", None, None),
        P("pole"),
    )
    return jax.shard_map(
        per_device, mesh=mesh, in_specs=placed, out_specs=P(("sub", "pole"), None), check_vma=False
    )
```

```python
import functools
import math

import jax
import jax.numpy as jnp
from jax import lax
from jax.experimental import pallas as pl
from jax.experimental.pallas import tpu as pltpu
from jax.sharding import PartitionSpec as P

f32 = jnp.float32
bf16 = jnp.bfloat16


def split(x):
    high = x.astype(bf16)
    low = (x - high.astype(f32)).astype(bf16)
    return high, low


def mm(a, b):
    return jnp.dot(a, b, preferred_element_type=f32)


def split_dot(a, b):
    width = b.shape[1]
    both = jnp.concatenate(split(b), axis=1)
    both = mm(a[0], both) + mm(a[1], both)
    return both[:, :width] + both[:, width:]


def turn(x):
    return pltpu.roll(x, x.shape[1] // 2, 1)


def left_lanes(x):
    return lax.broadcasted_iota(jnp.int32, x.shape, 1) < x.shape[1] // 2


def pack(top, bottom, half):
    if half == 0:
        return jnp.where(left_lanes(top), top, turn(bottom))
    return jnp.where(left_lanes(top), turn(top), bottom)


def sub_parity():
    return lax.rem(lax.axis_index("sub"), 2)


def pack_side(side_ref, s, half):
    rows = side_ref.shape[1] // 2
    return pack(side_ref[s, :rows, :], side_ref[s, rows:, :], half)


def gather_side(s, side, pass_ref, rows, side_ref, out_ref):
    for k in range(rows.shape[2]):
        side_ref[s, k : k + 1, :] = pass_ref[s, pl.ds(rows[s, side, k], 1), :]
    out_ref[s] = pack_side(side_ref, s, 0)


def first_kernel(weight, inv_hbm, field_hbm, rows_hbm, pass_ref, side_ref, off_ref, inv_buf,
                 field_buf, rows, inv_sems, field_sems, rows_sem):
    count = field_buf.shape[0]
    rows_copy = pltpu.make_async_copy(rows_hbm, rows, rows_sem)
    rows_copy.start()

    def copies(s):
        return (
            pltpu.make_async_copy(field_hbm.at[s], field_buf.at[s], field_sems.at[s]),
            pltpu.make_async_copy(inv_hbm.at[s], inv_buf.at[s], inv_sems.at[s]),
        )

    for s in range(count):
        for copy in copies(s):
            copy.start()
    rows_copy.wait()
    parity = sub_parity()

    def one_sub(s, carry):
        for copy in copies(s):
            copy.wait()
        gather_side(jnp.maximum(s - 1, 0), parity, pass_ref, rows, side_ref, off_ref)
        pass_ref[s] = weight[0] * split_dot(split(inv_buf[s]), field_buf[s])
        return carry

    lax.fori_loop(0, count, one_sub, 0)
    gather_side(count - 1, parity, pass_ref, rows, side_ref, off_ref)


def columns_kernel(rows_hbm, inv_ref, rows_ref, coup_ref, near_ref, pass_ref, off_side_ref,
                   high_cols_ref, low_cols_ref, pass0_ref, pass1_ref, off_ref, on0_ref, on1_ref, table_ref,
                   on_side_ref, rows, rows_sem):
    count, block_len = inv_ref.shape[:2]
    iface_len = rows_ref.shape[2]
    quarter = block_len // 4

    rows_copy = pltpu.make_async_copy(rows_hbm, rows, rows_sem)
    rows_copy.start()
    parity = sub_parity()
    for spot, side in enumerate((parity, 1 - parity)):
        near = lax.rem(near_ref[pl.ds(side, 1), :], count)
        for s in range(count):
            table_ref[spot, s] = jnp.broadcast_to(near[:, s : s + 1], table_ref.shape[2:])
    place = lax.broadcasted_iota(jnp.int32, (block_len, 2 * iface_len), 0)
    rows_copy.wait()

    def one_sub(s, carry):
        gather_side(s, 1 - parity, pass_ref, rows, on_side_ref, on0_ref)
        on1_ref[s] = pack_side(on_side_ref, s, 1)
        off_ref[s] = pack_side(off_side_ref, s, 1)
        for half, out_ref in enumerate((pass0_ref, pass1_ref)):
            for way in range(2):
                at = 2 * way * quarter
                out_ref[s, way] = pack(
                    pass_ref[s, at : at + quarter, :], pass_ref[s, at + quarter : at + 2 * quarter, :], half
                )
        at, coup = (
            jnp.concatenate([ref[s, pl.ds(side, 1), :] for side in (parity, 1 - parity)], axis=1)
            for ref in (rows_ref, coup_ref)
        )
        pick = (at == place).astype(f32).astype(bf16)
        inv_high, inv_low = split(inv_ref[s])
        high_cols_ref[s], low_cols_ref[s] = split((mm(inv_high, pick) + mm(inv_low, pick)) * coup)
        return carry

    lax.fori_loop(0, count, one_sub, 0)


def second_kernel(poles, sent, table_ref, high_ref, low_ref, pass_ref, off_ref, on_ref, out_ref):
    count, ways, quarter, _ = pass_ref.shape
    per_owner = count // poles
    steps = poles.bit_length() - 1
    me, parity = lax.axis_index("pole"), sub_parity()
    for r in range(sent, poles, 2):
        turned = sum(1 << (steps - 1 - step) for step in range(steps) if r >> step & 1)
        owner = me ^ jnp.where(parity == 0, r, turned)
        for c in range(per_owner):
            sub = owner * per_owner + c
            terms = []
            for spot, ref in enumerate((off_ref, on_ref)):
                near = jnp.concatenate([table_ref[spot, sub]] * (ref.shape[1] // 8), axis=0)
                side = ref[0]
                for at in range(1, count):
                    side = jnp.where(near == at, ref[at], side)
                turned_side = turn(side)
                terms += [
                    jnp.where(left_lanes(side), side, turned_side),
                    jnp.where(left_lanes(side), turned_side, side),
                ]
            terms = jnp.concatenate(terms, axis=0)
            high = terms.astype(bf16).astype(f32)
            both = jnp.where(left_lanes(terms), high, terms - high).astype(bf16)
            out = mm(high_ref[sub], both) + mm(low_ref[sub], both)
            out = out + turn(out)
            for way in range(ways):
                at = 2 * way * quarter
                top, bottom = out[at : at + quarter], out[at + quarter : at + 2 * quarter]
                to = (c * ways + way) * quarter
                out_ref[r // 2, to : to + quarter, :] = (
                    jnp.where(left_lanes(top), top, bottom) + pass_ref[sub, way]
                )


def gram_kernel(groups, per_owner, *refs):
    count = sum(groups)
    ins, (halves_ref, gram_ref, out_ref) = refs[:count], refs[count:]
    parts = []
    at = 0
    for size in groups:
        parts.append(functools.reduce(jnp.add, [ref[0] for ref in ins[at : at + size]]))
        at += size
    quarter = out_ref.shape[0] // (4 * per_owner)
    for way in range(2):
        for c in range(per_owner):
            first, second = (part[(2 * c + way) * quarter : (2 * c + way + 1) * quarter] for part in parts)
            at = (4 * c + 2 * way) * quarter
            out_ref[at : at + quarter, :] = jnp.where(left_lanes(first), first, turn(second))
            out_ref[at + quarter : at + 2 * quarter, :] = jnp.where(left_lanes(first), turn(first), second)
    high, low = split(out_ref[...])
    width = out_ref.shape[1]
    halves = jnp.concatenate([high, low], axis=1)
    halves_ref[...] = halves
    both = lax.dot_general(high, halves, (((0,), (0,)), ((), ())), preferred_element_type=f32)
    cross = both[:, width:]
    gram = both[:, :width] + (cross + cross.T)
    half = width // 2
    row = lax.broadcasted_iota(jnp.int32, (half, width), 0)
    col = lax.broadcasted_iota(jnp.int32, (half, width), 1)
    gram_ref[:half, :] = jnp.where(row > col - half, jnp.where(col < half, gram[half:], turn(gram[:half])), gram[half:])
    diag = jnp.sum(jnp.where(row == col, gram[:half], 0.0), axis=0, keepdims=True)
    gram_ref[half:, :] = jnp.broadcast_to(diag, (gram_ref.shape[0] - half, width))


def unpacked(gram):
    width = gram.shape[1]
    half = width // 2
    row = lax.broadcasted_iota(jnp.int32, (half, width), 0)
    col = lax.broadcasted_iota(jnp.int32, (half, width), 1)
    top = gram[:half]
    diag = jnp.broadcast_to(gram[half : half + 1], top.shape)
    first = jnp.where(row > col, turn(top), jnp.where(row == col, 0.5 * diag, 0.0))
    last = jnp.where(col < half, top, jnp.where(col - half > row, top, jnp.where(col - half == row, 0.5 * top, 0.0)))
    lower = jnp.concatenate([first, last], axis=0)
    return lower + lower.T


def reciprocal(x):
    guess = pl.reciprocal(x, approx=True)
    return guess * (2.0 - x * guess)


def four_pivots(a):
    det = a[0][0] * a[1][1] - a[1][0] * a[1][0]
    inv = reciprocal(det)
    p00, p01, p11 = a[1][1] * inv, -a[1][0] * inv, a[0][0] * inv
    g20, g21 = a[2][0] * p00 + a[2][1] * p01, a[2][0] * p01 + a[2][1] * p11
    g30, g31 = a[3][0] * p00 + a[3][1] * p01, a[3][0] * p01 + a[3][1] * p11
    s22 = a[2][2] - (g20 * a[2][0] + g21 * a[2][1])
    s32 = a[3][2] - (g30 * a[2][0] + g31 * a[2][1])
    s33 = a[3][3] - (g30 * a[3][0] + g31 * a[3][1])
    inv = reciprocal(s22 * s33 - s32 * s32)
    q00, q01, q11 = s33 * inv, -s32 * inv, s22 * inv

    def solve(r):
        z2 = r[2] - (g20 * r[0] + g21 * r[1])
        z3 = r[3] - (g30 * r[0] + g31 * r[1])
        w2, w3 = q00 * z2 + q01 * z3, q01 * z2 + q11 * z3
        w0 = p00 * r[0] + p01 * r[1] - (g20 * w2 + g30 * w3)
        w1 = p01 * r[0] + p11 * r[1] - (g21 * w2 + g31 * w3)
        return [w0, w1, w2, w3]

    def normalized(r):
        z2 = r[2] - (g20 * r[0] + g21 * r[1])
        z3 = r[3] - (g30 * r[0] + g31 * r[1])
        root0, root2 = lax.rsqrt(a[0][0]), lax.rsqrt(s22)
        l10, l32 = a[1][0] * (root0 * root0), s32 * (root2 * root2)
        return [
            r[0] * root0,
            (r[1] - l10 * r[0]) * lax.rsqrt(a[1][1] - l10 * a[1][0]),
            z2 * root2,
            (z3 - l32 * z2) * lax.rsqrt(s33 - l32 * s32),
        ]

    return solve, normalized


def combined(weights, rows):
    return (weights[0] * rows[0] + weights[1] * rows[1]) + (weights[2] * rows[2] + weights[3] * rows[3])


def inverse_rows(gram, tile_refs):
    vecs = gram.shape[0]
    tile, block = 8, 4
    tiles = vecs // tile
    sub_id = lax.broadcasted_iota(jnp.int32, (tile, vecs), 0)
    lane_id = lax.broadcasted_iota(jnp.int32, (tile, vecs), 1)
    diag = [jnp.where(lane_id == sub_id + t * tile, gram[t * tile : (t + 1) * tile], 0.0) for t in range(tiles)]
    scale = lax.rsqrt(jnp.sum(functools.reduce(jnp.add, diag), axis=0, keepdims=True))
    left, right = [], []
    for t in range(tiles):
        own = lax.rsqrt(jnp.sum(diag[t], axis=1, keepdims=True))
        left.append(gram[t * tile : (t + 1) * tile] * scale * own)
        right.append(jnp.where(lane_id == sub_id + t * tile, jnp.broadcast_to(scale, (tile, vecs)), 0.0))

    def lane(x, k):
        return jnp.broadcast_to(x[:, k : k + 1], (tile, vecs))

    def rows_of(tiles_now):
        for ref, x in zip(tile_refs, tiles_now):
            ref[...] = x
        return [[ref[pl.ds(i, tile, stride=0), :] for i in range(tile)] for ref in tile_refs]

    done = []
    for at in range(tiles):
        k = at * tile
        both_rows = rows_of((left[at], right[at]))
        a = [[lane(both_rows[0][i], k + j) for i in range(j + 1)] for j in range(tile)]
        solve, normalized = four_pivots(a)
        inner = [solve(a[j][:block]) for j in range(block, tile)]
        after = [
            [a[block + j][block + i] - combined(a[block + j], inner[i]) for i in range(j + 1)] for j in range(block)
        ]
        solve_after, normalized_after = four_pivots(after)
        weights = []
        for rows in both_rows:
            first = solve(rows[:block])
            later = [rows[block + j] - combined(a[block + j], first) for j in range(block)]
            second = solve_after(later)
            first = [w - combined([inner[j][i] for j in range(block)], second) for i, w in enumerate(first)]
            weights.append(first + second)
        done += [x[:1] for x in normalized(rows[:block]) + normalized_after(later)]
        for t in range(at + 1, tiles):
            cols = [lane(left[t], k + i) for i in range(tile)]
            for part, w in zip((left, right), weights):
                part[t] = part[t] - (combined(cols[:block], w[:block]) + combined(cols[block:], w[block:]))
    return jnp.concatenate(done, axis=0)


def ortho_kernel(scale, *refs):
    *gram_refs, halves_ref, out_ref, left_ref, right_ref = refs
    gram = functools.reduce(jnp.add, [ref[...] for ref in gram_refs])
    width = gram.shape[1]
    inverse = jnp.concatenate(split(inverse_rows(unpacked(gram), (left_ref, right_ref)) * scale), axis=0)
    both = lax.dot_general(
        halves_ref[...],
        jnp.concatenate([inverse, inverse], axis=1),
        (((1,), (1,)), ((), ())),
        preferred_element_type=f32,
    )
    out_ref[...] = both[:, :width] + both[:, width:]


def call(body, out_shape, flops=0, moved=0, limit=24, **kw):
    return pl.pallas_call(
        body,
        out_shape=out_shape,
        compiler_params=pltpu.CompilerParams(vmem_limit_bytes=limit * 1024 * 1024),
        cost_estimate=pl.CostEstimate(flops=flops, bytes_accessed=moved, transcendentals=0),
        **kw,
    )


def swap(value, even, odd):
    poles, groups = lax.axis_size("pole"), lax.axis_size("sub")
    pairs = []
    for p in range(poles):
        for s in range(groups):
            pole_mask, sub_mask = odd if s % 2 else even
            pairs.append((p * groups + s, (p ^ pole_mask) * groups + (s ^ sub_mask)))
    return lax.ppermute(value, ("pole", "sub"), pairs)


def per_device(start_block, inverses, iface_rows, neighbors, couplings, pole_weights):
    blocks = inverses[0]
    sub_count, block_len = blocks.shape[:2]
    vecs = start_block.shape[1]
    iface_len = iface_rows.shape[2]
    poles, groups = lax.axis_size("pole"), lax.axis_size("sub")
    fields = start_block.reshape(sub_count, block_len, vecs)
    shape = jax.ShapeDtypeStruct
    smem = pl.BlockSpec(memory_space=pltpu.SMEM)
    hbm = pl.BlockSpec(memory_space=pltpu.HBM)
    vmem = pl.BlockSpec(memory_space=pltpu.VMEM)
    block_bytes = sub_count * block_len * block_len * 4
    field_bytes = sub_count * block_len * vecs * 4
    packed = shape((sub_count, iface_len // 2, vecs), f32)
    in_hbm = functools.partial(pltpu.with_memory_space_constraint, memory_space=pltpu.HBM)
    in_vmem = functools.partial(pltpu.with_memory_space_constraint, memory_space=pltpu.VMEM)
    sides = shape((sub_count, iface_len, vecs), f32)
    first, off_side, off0, inv_here = call(
        first_kernel,
        (shape(fields.shape, f32), sides, packed, shape(blocks.shape, f32)),
        flops=8 * sub_count * block_len * block_len * vecs,
        moved=block_bytes + 3 * field_bytes,
        in_specs=[smem] + [hbm] * 3,
        out_specs=[vmem] * 4,
        scratch_shapes=[
            pltpu.VMEM(fields.shape, f32),
            pltpu.SMEM(iface_rows.shape, jnp.int32),
            pltpu.SemaphoreType.DMA((sub_count,)),
            pltpu.SemaphoreType.DMA((sub_count,)),
            pltpu.SemaphoreType.DMA,
        ],
        name="first_pass",
    )(pole_weights, *[in_hbm(v) for v in (blocks, fields, iface_rows)])
    first, off_side, inv_here = (in_vmem(v) for v in (first, off_side, inv_here))
    across = [(s, (s + (1 if s % 2 else -1)) % groups) for s in range(groups)]
    inside = [(s, s ^ 1) for s in range(groups)]
    off_in0 = lax.ppermute(off0, "sub", across)
    cols = shape((sub_count, block_len, 2 * iface_len), bf16)
    pass_half = shape((sub_count, 2, block_len // 4, vecs), f32)
    cols_high, cols_low, pass0, pass1, off1, on0, on1, table = call(
        columns_kernel,
        (cols, cols, pass_half, pass_half, packed, packed, packed, shape((2, sub_count, 8, vecs), jnp.int32)),
        flops=8 * sub_count * block_len * block_len * iface_len,
        moved=2 * block_bytes,
        in_specs=[hbm] + [vmem] * 6,
        out_specs=[vmem] * 8,
        scratch_shapes=[
            pltpu.VMEM(sides.shape, f32),
            pltpu.SMEM(iface_rows.shape, jnp.int32),
            pltpu.SemaphoreType.DMA,
        ],
        name="interface_columns",
    )(in_hbm(iface_rows), inv_here, iface_rows, couplings, neighbors.T, first, off_side)
    on_in0 = lax.ppermute(on0, "sub", inside)
    off1, on1, off_in0 = lax.optimization_barrier((off1, on1, off_in0))
    halves = [(off_in0, on_in0), (lax.ppermute(off1, "sub", across), lax.ppermute(on1, "sub", inside))]
    cols_high, cols_low, pass0, pass1 = (in_vmem(v) for v in (cols_high, cols_low, pass0, pass1))

    per_owner = sub_count // poles
    steps = poles.bit_length() - 1
    parts = shape((poles // 2, per_owner * block_len // 2, vecs), f32)
    pending = []
    for own_pass, (off_in, on_in) in zip((pass0, pass1), halves):
        send, keep = (
            call(
                functools.partial(second_kernel, poles, sent),
                parts,
                flops=4 * sub_count * block_len * 2 * iface_len * vecs,
                moved=2 * sub_count * block_len * vecs * 4,
                in_specs=[vmem] * 6,
                out_specs=vmem,
                name="second_pass",
            )(table, cols_high, cols_low, own_pass, off_in, on_in)
            for sent in (1, 0)
        )
        pending.append((send, [keep]))

    for step in range(steps):
        masks = (1 << step, 0), (1 << (steps - 1 - step), 0)
        for half, (send, kept) in enumerate(pending):
            kept = kept + [swap(send, *masks)]
            if kept[0].shape[0] > 1:
                send = functools.reduce(jnp.add, [v[1::2] for v in kept])
                kept = [v[0::2] for v in kept]
            pending[half] = (send, kept)

    summands = [kept for _, kept in pending]
    sizes = tuple(len(kept) for kept in summands)
    own_rows = per_owner * block_len
    basis_halves, gram = call(
        functools.partial(gram_kernel, sizes, per_owner),
        (shape((own_rows, 2 * vecs), bf16), shape((vecs // 2 + 8, vecs), f32)),
        flops=4 * own_rows * vecs * vecs,
        moved=5 * own_rows * vecs * 4,
        in_specs=[vmem] * sum(sizes),
        out_specs=[vmem] * 2,
        scratch_shapes=[pltpu.VMEM((own_rows, vecs), f32)],
        name="gram",
    )(*[v for kept in summands for v in kept])

    stages = [[(0, 1)], [(r, 0) for r in range(1, poles)]]
    base = 2
    while base < groups:
        radix = min(4, groups // base)
        stages.append([(0, base * r) for r in range(1, radix)])
        base *= radix
    grams = [gram]
    for masks in stages:
        total = functools.reduce(jnp.add, grams)
        grams = [total] + [swap(total, m, m) for m in masks]

    total_rows = sub_count * block_len * groups
    return call(
        functools.partial(ortho_kernel, math.sqrt(total_rows)),
        shape((own_rows, vecs), f32),
        flops=6 * own_rows * vecs * vecs,
        moved=2 * own_rows * vecs * 4,
        in_specs=[vmem] * (len(grams) + 1),
        out_specs=vmem,
        scratch_shapes=[pltpu.VMEM((8, vecs), f32)] * 2,
        name="ortho",
    )(*grams, basis_halves)


def solution(mesh):
    placed = (
        P("sub", None),
        P("pole", "sub", None, None),
        P("sub", None, None),
        P("sub", None),
        P("sub", None, None),
        P("pole"),
    )
    return jax.shard_map(
        per_device, mesh=mesh, in_specs=placed, out_specs=P(("sub", "pole"), None), check_vma=False
    )
```

```python
import functools
import itertools
import math

import jax
import jax.numpy as jnp
from jax import lax
from jax.experimental import pallas as pl
from jax.experimental.pallas import tpu as pltpu
from jax.sharding import PartitionSpec as P

f32 = jnp.float32
bf16 = jnp.bfloat16


def split(x):
    high = x.astype(bf16)
    low = (x - high.astype(f32)).astype(bf16)
    return high, low


def mm(a, b):
    return jnp.dot(a, b, preferred_element_type=f32)


def split_dot(a, b):
    width = b.shape[1]
    both = jnp.concatenate(split(b), axis=1)
    both = mm(a[0], both) + mm(a[1], both)
    return both[:, :width] + both[:, width:]


def turn(x):
    return pltpu.roll(x, x.shape[1] // 2, 1)


def left_lanes(x):
    return lax.broadcasted_iota(jnp.int32, x.shape, 1) < x.shape[1] // 2


def pack(top, bottom, half):
    if half == 0:
        return jnp.where(left_lanes(top), top, turn(bottom))
    return jnp.where(left_lanes(top), turn(top), bottom)


def sub_parity():
    return lax.rem(lax.axis_index("sub"), 2)


def pack_side(side_ref, s, half):
    rows = side_ref.shape[1] // 2
    return pack(side_ref[s, :rows, :], side_ref[s, rows:, :], half)


def gather_side(s, side, pass_ref, rows, side_ref, out_ref):
    for k in range(rows.shape[2]):
        side_ref[s, k : k + 1, :] = pass_ref[s, pl.ds(rows[s, side, k], 1), :]
    out_ref[s] = pack_side(side_ref, s, 0)


def first_kernel(weight, inv_hbm, field_hbm, rows_hbm, pass_ref, side_ref, off_ref, inv_high_ref, inv_low_ref,
                 inv_buf, field_buf, rows, inv_sems, field_sems, rows_sem):
    count = field_buf.shape[0]
    rows_copy = pltpu.make_async_copy(rows_hbm, rows, rows_sem)
    rows_copy.start()

    def copies(s):
        return (
            pltpu.make_async_copy(field_hbm.at[s], field_buf.at[s], field_sems.at[s]),
            pltpu.make_async_copy(inv_hbm.at[s], inv_buf.at[s], inv_sems.at[s]),
        )

    for s in range(count):
        for copy in copies(s):
            copy.start()
    rows_copy.wait()
    parity = sub_parity()

    def one_sub(s, carry):
        for copy in copies(s):
            copy.wait()
        gather_side(jnp.maximum(s - 1, 0), parity, pass_ref, rows, side_ref, off_ref)
        inv_high_ref[s], inv_low_ref[s] = parts = split(inv_buf[s])
        pass_ref[s] = weight[0] * split_dot(parts, field_buf[s])
        return carry

    lax.fori_loop(0, count, one_sub, 0)
    gather_side(count - 1, parity, pass_ref, rows, side_ref, off_ref)


def columns_kernel(rows_hbm, inv_high_ref, inv_low_ref, rows_ref, coup_ref, near_ref, pass_ref, off_side_ref,
                   high_cols_ref, low_cols_ref, pass0_ref, pass1_ref, off_ref, on0_ref, on1_ref, table_ref,
                   on_side_ref, rows, rows_sem):
    count, block_len = inv_high_ref.shape[:2]
    iface_len = rows_ref.shape[2]
    quarter = block_len // 4

    rows_copy = pltpu.make_async_copy(rows_hbm, rows, rows_sem)
    rows_copy.start()
    parity = sub_parity()
    for spot, side in enumerate((parity, 1 - parity)):
        near = lax.rem(near_ref[pl.ds(side, 1), :], count)
        for s in range(count):
            table_ref[spot, s] = jnp.broadcast_to(near[:, s : s + 1], table_ref.shape[2:])
    place = lax.broadcasted_iota(jnp.int32, (block_len, 2 * iface_len), 0)
    rows_copy.wait()

    def one_sub(s, carry):
        gather_side(s, 1 - parity, pass_ref, rows, on_side_ref, on0_ref)
        on1_ref[s] = pack_side(on_side_ref, s, 1)
        off_ref[s] = pack_side(off_side_ref, s, 1)
        for half, out_ref in enumerate((pass0_ref, pass1_ref)):
            for way in range(2):
                at = 2 * way * quarter
                out_ref[s, way] = pack(
                    pass_ref[s, at : at + quarter, :], pass_ref[s, at + quarter : at + 2 * quarter, :], half
                )
        at, coup = (
            jnp.concatenate([ref[s, pl.ds(side, 1), :] for side in (parity, 1 - parity)], axis=1)
            for ref in (rows_ref, coup_ref)
        )
        pick = (at == place).astype(f32).astype(bf16)
        high_cols_ref[s], low_cols_ref[s] = split((mm(inv_high_ref[s], pick) + mm(inv_low_ref[s], pick)) * coup)
        return carry

    lax.fori_loop(0, count, one_sub, 0)


def second_kernel(poles, sent, table_ref, high_ref, low_ref, pass_ref, off_ref, on_ref, *out_refs):
    count, ways, quarter, _ = pass_ref.shape
    per_owner = count // poles
    steps = poles.bit_length() - 1
    me, parity = lax.axis_index("pole"), sub_parity()
    split_ways = len(out_refs) == ways
    for r in range(sent, poles, 2):
        turned = sum(1 << (steps - 1 - step) for step in range(steps) if r >> step & 1)
        if split_ways:
            owners = [(me ^ r, [0]), (me ^ turned, [1])]
        else:
            owners = [(me ^ jnp.where(parity == 0, r, turned), [0, 1])]
        for c in range(per_owner):
            for owner, own_ways in owners:
                sub = owner * per_owner + c
                terms = []
                for spot, ref in enumerate((off_ref, on_ref)):
                    near = jnp.concatenate([table_ref[spot, sub]] * (ref.shape[1] // 8), axis=0)
                    side = ref[0]
                    for at in range(1, count):
                        side = jnp.where(near == at, ref[at], side)
                    turned_side = turn(side)
                    terms += [
                        jnp.where(left_lanes(side), side, turned_side),
                        jnp.where(left_lanes(side), turned_side, side),
                    ]
                terms = jnp.concatenate(terms, axis=0)
                high = terms.astype(bf16).astype(f32)
                both = jnp.where(left_lanes(terms), high, terms - high).astype(bf16)
                start, stop = 2 * own_ways[0] * quarter, 2 * (own_ways[-1] + 1) * quarter
                out = mm(high_ref[sub, start:stop, :], both) + mm(low_ref[sub, start:stop, :], both)
                out = out + turn(out)
                for spot, way in enumerate(own_ways):
                    at = 2 * spot * quarter
                    top, bottom = out[at : at + quarter], out[at + quarter : at + 2 * quarter]
                    to = (c * len(own_ways) + spot) * quarter
                    out_refs[way if split_ways else 0][r // 2, to : to + quarter, :] = (
                        jnp.where(left_lanes(top), top, bottom) + pass_ref[sub, way]
                    )


def gram_kernel(halves, per_owner, *refs):
    count = sum(size for sizes in halves for size in sizes)
    ins, (halves_ref, gram_ref, out_ref) = refs[:count], refs[count:]
    parts = []
    at = 0
    for sizes in halves:
        parts.append([])
        for size in sizes:
            parts[-1].append(functools.reduce(jnp.add, [ref[0] for ref in ins[at : at + size]]))
            at += size
    quarter = out_ref.shape[0] // (4 * per_owner)

    def piece(arrays, c, way):
        spot = c if len(arrays) == 2 else 2 * c + way
        return arrays[way % len(arrays)][spot * quarter : (spot + 1) * quarter]

    for way in range(2):
        for c in range(per_owner):
            first, second = (piece(arrays, c, way) for arrays in parts)
            at = (4 * c + 2 * way) * quarter
            out_ref[at : at + quarter, :] = jnp.where(left_lanes(first), first, turn(second))
            out_ref[at + quarter : at + 2 * quarter, :] = jnp.where(left_lanes(first), turn(first), second)
    high, low = split(out_ref[...])
    width = out_ref.shape[1]
    halves = jnp.concatenate([high, low], axis=1)
    halves_ref[...] = halves
    both = lax.dot_general(high, halves, (((0,), (0,)), ((), ())), preferred_element_type=f32)
    cross = both[:, width:]
    gram = both[:, :width] + (cross + cross.T)
    half = width // 2
    row = lax.broadcasted_iota(jnp.int32, (half, width), 0)
    col = lax.broadcasted_iota(jnp.int32, (half, width), 1)
    gram_ref[:half, :] = jnp.where(row > col - half, jnp.where(col < half, gram[half:], turn(gram[:half])), gram[half:])
    diag = jnp.sum(jnp.where(row == col, gram[:half], 0.0), axis=0, keepdims=True)
    gram_ref[half:, :] = jnp.broadcast_to(diag, (gram_ref.shape[0] - half, width))


def share_kernel(total_ref, *refs):
    *got_refs, out_ref = refs
    own = jnp.where(sub_parity() == 0, total_ref[...], 0.0)
    out_ref[...] = functools.reduce(jnp.add, [ref[...] for ref in got_refs], own)


def unpacked(gram):
    width = gram.shape[1]
    half = width // 2
    row = lax.broadcasted_iota(jnp.int32, (half, width), 0)
    col = lax.broadcasted_iota(jnp.int32, (half, width), 1)
    top = gram[:half]
    diag = jnp.broadcast_to(gram[half : half + 1], top.shape)
    first = jnp.where(row > col, turn(top), jnp.where(row == col, 0.5 * diag, 0.0))
    last = jnp.where(col < half, top, jnp.where(col - half > row, top, jnp.where(col - half == row, 0.5 * top, 0.0)))
    lower = jnp.concatenate([first, last], axis=0)
    return lower + lower.T


def four_pivots(a):
    det = a[0][0] * a[1][1] - a[1][0] * a[1][0]
    inv = 1.0 / det
    p00, p01, p11 = a[1][1] * inv, -a[1][0] * inv, a[0][0] * inv
    g20, g21 = a[2][0] * p00 + a[2][1] * p01, a[2][0] * p01 + a[2][1] * p11
    g30, g31 = a[3][0] * p00 + a[3][1] * p01, a[3][0] * p01 + a[3][1] * p11
    s22 = a[2][2] - (g20 * a[2][0] + g21 * a[2][1])
    s32 = a[3][2] - (g30 * a[2][0] + g31 * a[2][1])
    s33 = a[3][3] - (g30 * a[3][0] + g31 * a[3][1])
    inv = 1.0 / (s22 * s33 - s32 * s32)
    q00, q01, q11 = s33 * inv, -s32 * inv, s22 * inv

    def solve(r):
        z2 = r[2] - (g20 * r[0] + g21 * r[1])
        z3 = r[3] - (g30 * r[0] + g31 * r[1])
        w2, w3 = q00 * z2 + q01 * z3, q01 * z2 + q11 * z3
        w0 = p00 * r[0] + p01 * r[1] - (g20 * w2 + g30 * w3)
        w1 = p01 * r[0] + p11 * r[1] - (g21 * w2 + g31 * w3)
        return [w0, w1, w2, w3]

    def normalized(r):
        z2 = r[2] - (g20 * r[0] + g21 * r[1])
        z3 = r[3] - (g30 * r[0] + g31 * r[1])
        root0, root2 = lax.rsqrt(a[0][0]), lax.rsqrt(s22)
        l10, l32 = a[1][0] * (root0 * root0), s32 * (root2 * root2)
        return [
            r[0] * root0,
            (r[1] - l10 * r[0]) * lax.rsqrt(a[1][1] - l10 * a[1][0]),
            z2 * root2,
            (z3 - l32 * z2) * lax.rsqrt(s33 - l32 * s32),
        ]

    return solve, normalized


def combined(weights, rows):
    return (weights[0] * rows[0] + weights[1] * rows[1]) + (weights[2] * rows[2] + weights[3] * rows[3])


def inverse_rows(gram, tile_refs):
    vecs = gram.shape[0]
    tile, block = 8, 4
    tiles = vecs // tile
    sub_id = lax.broadcasted_iota(jnp.int32, (tile, vecs), 0)
    lane_id = lax.broadcasted_iota(jnp.int32, (tile, vecs), 1)
    diag = [jnp.where(lane_id == sub_id + t * tile, gram[t * tile : (t + 1) * tile], 0.0) for t in range(tiles)]
    scale = lax.rsqrt(jnp.sum(functools.reduce(jnp.add, diag), axis=0, keepdims=True))
    left, right = [], []
    for t in range(tiles):
        own = lax.rsqrt(jnp.sum(diag[t], axis=1, keepdims=True))
        left.append(gram[t * tile : (t + 1) * tile] * scale * own)
        right.append(jnp.where(lane_id == sub_id + t * tile, jnp.broadcast_to(scale, (tile, vecs)), 0.0))

    def lane(x, k):
        return jnp.broadcast_to(x[:, k : k + 1], (tile, vecs))

    def rows_of(tiles_now):
        for ref, x in zip(tile_refs, tiles_now):
            ref[...] = x
        return [[ref[pl.ds(i, tile, stride=0), :] for i in range(tile)] for ref in tile_refs]

    done = []
    for at in range(tiles):
        k = at * tile
        both_rows = rows_of((left[at], right[at]))
        a = [[lane(both_rows[0][i], k + j) for i in range(j + 1)] for j in range(tile)]
        solve, normalized = four_pivots(a)
        inner = [solve(a[j][:block]) for j in range(block, tile)]
        after = [
            [a[block + j][block + i] - combined(a[block + j], inner[i]) for i in range(j + 1)] for j in range(block)
        ]
        solve_after, normalized_after = four_pivots(after)
        weights = []
        for rows in both_rows:
            first = solve(rows[:block])
            later = [rows[block + j] - combined(a[block + j], first) for j in range(block)]
            second = solve_after(later)
            first = [w - combined([inner[j][i] for j in range(block)], second) for i, w in enumerate(first)]
            weights.append(first + second)
        done += [x[:1] for x in normalized(rows[:block]) + normalized_after(later)]
        for t in range(at + 1, tiles):
            cols = [lane(left[t], k + i) for i in range(tile)]
            for part, w in zip((left, right), weights):
                part[t] = part[t] - (combined(cols[:block], w[:block]) + combined(cols[block:], w[block:]))
    return jnp.concatenate(done, axis=0)


def ortho_kernel(scale, *refs):
    *gram_refs, halves_ref, out_ref, left_ref, right_ref = refs
    gram = functools.reduce(jnp.add, [ref[...] for ref in gram_refs])
    width = gram.shape[1]
    inverse = jnp.concatenate(split(inverse_rows(unpacked(gram), (left_ref, right_ref)) * scale), axis=0)
    both = lax.dot_general(
        halves_ref[...],
        jnp.concatenate([inverse, inverse], axis=1),
        (((1,), (1,)), ((), ())),
        preferred_element_type=f32,
    )
    out_ref[...] = both[:, :width] + both[:, width:]


def call(body, out_shape, flops=0, moved=0, limit=24, **kw):
    return pl.pallas_call(
        body,
        out_shape=out_shape,
        compiler_params=pltpu.CompilerParams(vmem_limit_bytes=limit * 1024 * 1024),
        cost_estimate=pl.CostEstimate(flops=flops, bytes_accessed=moved, transcendentals=0),
        **kw,
    )


def swap(value, even, odd):
    poles, groups = lax.axis_size("pole"), lax.axis_size("sub")
    pairs = []
    for p in range(poles):
        for s in range(groups):
            masks = odd if s % 2 else even
            if masks:
                pairs.append((p * groups + s, (p ^ masks[0]) * groups + (s ^ masks[1])))
    return lax.ppermute(value, ("pole", "sub"), pairs)


def per_device(start_block, inverses, iface_rows, neighbors, couplings, pole_weights):
    blocks = inverses[0]
    sub_count, block_len = blocks.shape[:2]
    vecs = start_block.shape[1]
    iface_len = iface_rows.shape[2]
    poles, groups = lax.axis_size("pole"), lax.axis_size("sub")
    fields = start_block.reshape(sub_count, block_len, vecs)
    shape = jax.ShapeDtypeStruct
    smem = pl.BlockSpec(memory_space=pltpu.SMEM)
    hbm = pl.BlockSpec(memory_space=pltpu.HBM)
    vmem = pl.BlockSpec(memory_space=pltpu.VMEM)
    block_bytes = sub_count * block_len * block_len * 4
    field_bytes = sub_count * block_len * vecs * 4
    packed = shape((sub_count, iface_len // 2, vecs), f32)
    in_hbm = functools.partial(pltpu.with_memory_space_constraint, memory_space=pltpu.HBM)
    in_vmem = functools.partial(pltpu.with_memory_space_constraint, memory_space=pltpu.VMEM)
    sides = shape((sub_count, iface_len, vecs), f32)
    halves = shape(blocks.shape, bf16)
    first, off_side, off0, inv_high, inv_low = call(
        first_kernel,
        (shape(fields.shape, f32), sides, packed, halves, halves),
        flops=8 * sub_count * block_len * block_len * vecs,
        moved=block_bytes + 3 * field_bytes,
        in_specs=[smem] + [hbm] * 3,
        out_specs=[vmem] * 5,
        scratch_shapes=[
            pltpu.VMEM(blocks.shape, f32),
            pltpu.VMEM(fields.shape, f32),
            pltpu.SMEM(iface_rows.shape, jnp.int32),
            pltpu.SemaphoreType.DMA((sub_count,)),
            pltpu.SemaphoreType.DMA((sub_count,)),
            pltpu.SemaphoreType.DMA,
        ],
        name="first_pass",
    )(pole_weights, *[in_hbm(v) for v in (blocks, fields, iface_rows)])
    first, off_side, inv_high, inv_low = (in_vmem(v) for v in (first, off_side, inv_high, inv_low))
    across = [(s, (s + (1 if s % 2 else -1)) % groups) for s in range(groups)]
    inside = [(s, s ^ 1) for s in range(groups)]
    off_in0 = lax.ppermute(off0, "sub", across)
    cols = shape((sub_count, block_len, 2 * iface_len), bf16)
    pass_half = shape((sub_count, 2, block_len // 4, vecs), f32)
    cols_high, cols_low, pass0, pass1, off1, on0, on1, table = call(
        columns_kernel,
        (cols, cols, pass_half, pass_half, packed, packed, packed, shape((2, sub_count, 8, vecs), jnp.int32)),
        flops=8 * sub_count * block_len * block_len * iface_len,
        moved=2 * block_bytes,
        in_specs=[hbm] + [vmem] * 7,
        out_specs=[vmem] * 8,
        scratch_shapes=[
            pltpu.VMEM(sides.shape, f32),
            pltpu.SMEM(iface_rows.shape, jnp.int32),
            pltpu.SemaphoreType.DMA,
        ],
        name="interface_columns",
    )(in_hbm(iface_rows), inv_high, inv_low, iface_rows, couplings, neighbors.T, first, off_side)
    on_in0 = lax.ppermute(on0, "sub", inside)
    on1, off_in0 = lax.optimization_barrier((on1, off_in0))
    halves = [(off_in0, on_in0), (lax.ppermute(off1, "sub", across), lax.ppermute(on1, "sub", inside))]
    cols_high, cols_low, pass0, pass1 = (in_vmem(v) for v in (cols_high, cols_low, pass0, pass1))

    per_owner = sub_count // poles
    steps = poles.bit_length() - 1
    pending = []
    for arrays, own_pass, (off_in, on_in) in zip((1, 2), (pass0, pass1), halves):
        send, keep = (
            call(
                functools.partial(second_kernel, poles, sent),
                (shape((poles // 2, per_owner * block_len // (2 * arrays), vecs), f32),) * arrays,
                flops=4 * sub_count * block_len * 2 * iface_len * vecs,
                moved=2 * sub_count * block_len * vecs * 4,
                in_specs=[vmem] * 6,
                out_specs=[vmem] * arrays,
                name="second_pass",
            )(table, cols_high, cols_low, own_pass, off_in, on_in)
            for sent in (1, 0)
        )
        pending.append([(a, [b]) for a, b in zip(send, keep)])

    for step in range(steps):
        in_order, turned = (1 << step, 0), (1 << (steps - 1 - step), 0)
        for arrays in pending:
            for way, (send, kept) in enumerate(arrays):
                masks = (in_order, turned) if len(arrays) == 1 else ((in_order, turned)[way],) * 2
                kept = kept + [swap(send, *masks)]
                if kept[0].shape[0] > 1:
                    send = functools.reduce(jnp.add, [v[1::2] for v in kept])
                    kept = [v[0::2] for v in kept]
                arrays[way] = (send, kept)

    summands = [[kept for _, kept in arrays] for arrays in pending]
    sizes = tuple(tuple(len(kept) for kept in arrays) for arrays in summands)
    own_rows = per_owner * block_len
    basis_halves, gram = call(
        functools.partial(gram_kernel, sizes, per_owner),
        (shape((own_rows, 2 * vecs), bf16), shape((vecs // 2 + 8, vecs), f32)),
        flops=4 * own_rows * vecs * vecs,
        moved=5 * own_rows * vecs * 4,
        in_specs=[vmem] * sum(map(sum, sizes)),
        out_specs=[vmem] * 2,
        scratch_shapes=[pltpu.VMEM((own_rows, vecs), f32)],
        name="gram",
    )(*[v for arrays in summands for kept in arrays for v in kept])

    stages = [[(r, 0) for r in range(poles - 1, 0, -1)]]
    base = 2
    while base < groups:
        radix = min(4, groups // base)
        stages.append([(0, base * r) for r in range(radix - 1, 0, -1)])
        base *= radix
    inside_chip = ((0, 1), (0, 1))
    grams = [gram, swap(gram, *inside_chip)]
    for masks in stages:
        total = functools.reduce(jnp.add, grams)
        got = [
            swap(total, even, odd) for even, odd in itertools.zip_longest(masks[0::2], masks[1::2])
        ]
        share = call(share_kernel, shape(gram.shape, f32), name="gram_share")(total, *got)
        grams = [share, swap(share, *inside_chip)]

    total_rows = sub_count * block_len * groups
    return call(
        functools.partial(ortho_kernel, math.sqrt(total_rows)),
        shape((own_rows, vecs), f32),
        flops=6 * own_rows * vecs * vecs,
        moved=2 * own_rows * vecs * 4,
        in_specs=[vmem] * (len(grams) + 1),
        out_specs=vmem,
        scratch_shapes=[pltpu.VMEM((8, vecs), f32)] * 2,
        name="ortho",
    )(*grams, basis_halves)


def solution(mesh):
    placed = (
        P("sub", None),
        P("pole", "sub", None, None),
        P("sub", None, None),
        P("sub", None),
        P("sub", None, None),
        P("pole"),
    )
    return jax.shard_map(
        per_device, mesh=mesh, in_specs=placed, out_specs=P(("sub", "pole"), None), check_vma=False
    )
```

```python
import functools
import math

import jax
import jax.numpy as jnp
from jax import lax
from jax.experimental import pallas as pl
from jax.experimental.pallas import tpu as pltpu
from jax.sharding import PartitionSpec as P

f32 = jnp.float32
bf16 = jnp.bfloat16


def split(x):
    high = x.astype(bf16)
    low = (x - high.astype(f32)).astype(bf16)
    return high, low


def mm(a, b):
    return jnp.dot(a, b, preferred_element_type=f32)


def split_dot(a, b):
    width = b.shape[1]
    both = jnp.concatenate(split(b), axis=1)
    both = mm(a[0], both) + mm(a[1], both)
    return both[:, :width] + both[:, width:]


def turn(x):
    return pltpu.roll(x, x.shape[1] // 2, 1)


def left_lanes(x):
    return lax.broadcasted_iota(jnp.int32, x.shape, 1) < x.shape[1] // 2


def pack(top, bottom, half):
    if half == 0:
        return jnp.where(left_lanes(top), top, turn(bottom))
    return jnp.where(left_lanes(top), turn(top), bottom)


def sub_parity():
    return lax.rem(lax.axis_index("sub"), 2)


def pack_side(side_ref, s, half):
    rows = side_ref.shape[1] // 2
    return pack(side_ref[s, :rows, :], side_ref[s, rows:, :], half)


def gather_side(s, side, pass_ref, rows, side_ref, out_ref):
    for k in range(rows.shape[2]):
        side_ref[s, k : k + 1, :] = pass_ref[s, pl.ds(rows[s, side, k], 1), :]
    out_ref[s] = pack_side(side_ref, s, 0)


def first_kernel(weight, inv_hbm, field_hbm, rows_hbm, pass_ref, side_ref, off_ref, inv_high_ref, inv_low_ref,
                 inv_buf, field_buf, rows, inv_sems, field_sems, rows_sem):
    count = field_buf.shape[0]
    rows_copy = pltpu.make_async_copy(rows_hbm, rows, rows_sem)
    rows_copy.start()

    def copies(s):
        return (
            pltpu.make_async_copy(field_hbm.at[s], field_buf.at[s], field_sems.at[s]),
            pltpu.make_async_copy(inv_hbm.at[s], inv_buf.at[s], inv_sems.at[s]),
        )

    for s in range(count):
        for copy in copies(s):
            copy.start()
    rows_copy.wait()
    parity = sub_parity()

    def one_sub(s, carry):
        for copy in copies(s):
            copy.wait()
        gather_side(jnp.maximum(s - 1, 0), parity, pass_ref, rows, side_ref, off_ref)
        inv_high_ref[s], inv_low_ref[s] = parts = split(inv_buf[s])
        pass_ref[s] = weight[0] * split_dot(parts, field_buf[s])
        return carry

    lax.fori_loop(0, count, one_sub, 0)
    gather_side(count - 1, parity, pass_ref, rows, side_ref, off_ref)


def columns_kernel(rows_hbm, inv_high_ref, inv_low_ref, rows_ref, coup_ref, near_ref, pass_ref, off_side_ref,
                   high_cols_ref, low_cols_ref, pass0_ref, pass1_ref, off_ref, on0_ref, on1_ref, table_ref,
                   on_side_ref, rows, rows_sem):
    count, block_len = inv_high_ref.shape[:2]
    iface_len = rows_ref.shape[2]
    quarter = block_len // 4

    rows_copy = pltpu.make_async_copy(rows_hbm, rows, rows_sem)
    rows_copy.start()
    parity = sub_parity()
    for spot, side in enumerate((parity, 1 - parity)):
        near = lax.rem(near_ref[pl.ds(side, 1), :], count)
        for s in range(count):
            table_ref[spot, s] = jnp.broadcast_to(near[:, s : s + 1], table_ref.shape[2:])
    place = lax.broadcasted_iota(jnp.int32, (block_len, 2 * iface_len), 0)
    rows_copy.wait()

    def one_sub(s, carry):
        gather_side(s, 1 - parity, pass_ref, rows, on_side_ref, on0_ref)
        on1_ref[s] = pack_side(on_side_ref, s, 1)
        off_ref[s] = pack_side(off_side_ref, s, 1)
        for half, out_ref in enumerate((pass0_ref, pass1_ref)):
            for way in range(2):
                at = 2 * way * quarter
                out_ref[s, way] = pack(
                    pass_ref[s, at : at + quarter, :], pass_ref[s, at + quarter : at + 2 * quarter, :], half
                )
        at, coup = (
            jnp.concatenate([ref[s, pl.ds(side, 1), :] for side in (parity, 1 - parity)], axis=1)
            for ref in (rows_ref, coup_ref)
        )
        pick = (at == place).astype(f32).astype(bf16)
        high_cols_ref[s], low_cols_ref[s] = split((mm(inv_high_ref[s], pick) + mm(inv_low_ref[s], pick)) * coup)
        return carry

    lax.fori_loop(0, count, one_sub, 0)


def second_kernel(poles, sent, table_ref, high_ref, low_ref, pass_ref, off_ref, on_ref, *out_refs):
    count, ways, quarter, _ = pass_ref.shape
    per_owner = count // poles
    steps = poles.bit_length() - 1
    me, parity = lax.axis_index("pole"), sub_parity()
    split_ways = len(out_refs) == ways
    for r in range(sent, poles, 2):
        turned = sum(1 << (steps - 1 - step) for step in range(steps) if r >> step & 1)
        if split_ways:
            owners = [(me ^ r, [0]), (me ^ turned, [1])]
        else:
            owners = [(me ^ jnp.where(parity == 0, r, turned), [0, 1])]
        for c in range(per_owner):
            for owner, own_ways in owners:
                sub = owner * per_owner + c
                terms = []
                for spot, ref in enumerate((off_ref, on_ref)):
                    near = jnp.concatenate([table_ref[spot, sub]] * (ref.shape[1] // 8), axis=0)
                    side = ref[0]
                    for at in range(1, count):
                        side = jnp.where(near == at, ref[at], side)
                    turned_side = turn(side)
                    terms += [
                        jnp.where(left_lanes(side), side, turned_side),
                        jnp.where(left_lanes(side), turned_side, side),
                    ]
                terms = jnp.concatenate(terms, axis=0)
                high = terms.astype(bf16).astype(f32)
                both = jnp.where(left_lanes(terms), high, terms - high).astype(bf16)
                start, stop = 2 * own_ways[0] * quarter, 2 * (own_ways[-1] + 1) * quarter
                out = mm(high_ref[sub, start:stop, :], both) + mm(low_ref[sub, start:stop, :], both)
                out = out + turn(out)
                for spot, way in enumerate(own_ways):
                    at = 2 * spot * quarter
                    top, bottom = out[at : at + quarter], out[at + quarter : at + 2 * quarter]
                    to = (c * len(own_ways) + spot) * quarter
                    out_refs[way if split_ways else 0][r // 2, to : to + quarter, :] = (
                        jnp.where(left_lanes(top), top, bottom) + pass_ref[sub, way]
                    )


def gram_kernel(halves, per_owner, *refs):
    count = sum(size for sizes in halves for size in sizes)
    ins, (halves_ref, gram_ref, out_ref) = refs[:count], refs[count:]
    parts = []
    at = 0
    for sizes in halves:
        parts.append([])
        for size in sizes:
            parts[-1].append(functools.reduce(jnp.add, [ref[0] for ref in ins[at : at + size]]))
            at += size
    quarter = out_ref.shape[0] // (4 * per_owner)

    def piece(arrays, c, way):
        spot = c if len(arrays) == 2 else 2 * c + way
        return arrays[way % len(arrays)][spot * quarter : (spot + 1) * quarter]

    for way in range(2):
        for c in range(per_owner):
            first, second = (piece(arrays, c, way) for arrays in parts)
            at = (4 * c + 2 * way) * quarter
            out_ref[at : at + quarter, :] = jnp.where(left_lanes(first), first, turn(second))
            out_ref[at + quarter : at + 2 * quarter, :] = jnp.where(left_lanes(first), turn(first), second)
    high, low = split(out_ref[...])
    width = out_ref.shape[1]
    halves = jnp.concatenate([high, low], axis=1)
    halves_ref[...] = halves
    both = lax.dot_general(high, halves, (((0,), (0,)), ((), ())), preferred_element_type=f32)
    cross = both[:, width:]
    gram = both[:, :width] + (cross + cross.T)
    half = width // 2
    row = lax.broadcasted_iota(jnp.int32, (half, width), 0)
    col = lax.broadcasted_iota(jnp.int32, (half, width), 1)
    gram_ref[:half, :] = jnp.where(row > col - half, jnp.where(col < half, gram[half:], turn(gram[:half])), gram[half:])
    diag = jnp.sum(jnp.where(row == col, gram[:half], 0.0), axis=0, keepdims=True)
    gram_ref[half:, :] = jnp.broadcast_to(diag, (gram_ref.shape[0] - half, width))


def unpacked(gram):
    width = gram.shape[1]
    half = width // 2
    row = lax.broadcasted_iota(jnp.int32, (half, width), 0)
    col = lax.broadcasted_iota(jnp.int32, (half, width), 1)
    top = gram[:half]
    diag = jnp.broadcast_to(gram[half : half + 1], top.shape)
    first = jnp.where(row > col, turn(top), jnp.where(row == col, 0.5 * diag, 0.0))
    last = jnp.where(col < half, top, jnp.where(col - half > row, top, jnp.where(col - half == row, 0.5 * top, 0.0)))
    lower = jnp.concatenate([first, last], axis=0)
    return lower + lower.T


def four_pivots(a):
    det = a[0][0] * a[1][1] - a[1][0] * a[1][0]
    inv = 1.0 / det
    p00, p01, p11 = a[1][1] * inv, -a[1][0] * inv, a[0][0] * inv
    g20, g21 = a[2][0] * p00 + a[2][1] * p01, a[2][0] * p01 + a[2][1] * p11
    g30, g31 = a[3][0] * p00 + a[3][1] * p01, a[3][0] * p01 + a[3][1] * p11
    s22 = a[2][2] - (g20 * a[2][0] + g21 * a[2][1])
    s32 = a[3][2] - (g30 * a[2][0] + g31 * a[2][1])
    s33 = a[3][3] - (g30 * a[3][0] + g31 * a[3][1])
    inv = 1.0 / (s22 * s33 - s32 * s32)
    q00, q01, q11 = s33 * inv, -s32 * inv, s22 * inv

    def solve(r):
        z2 = r[2] - (g20 * r[0] + g21 * r[1])
        z3 = r[3] - (g30 * r[0] + g31 * r[1])
        w2, w3 = q00 * z2 + q01 * z3, q01 * z2 + q11 * z3
        w0 = p00 * r[0] + p01 * r[1] - (g20 * w2 + g30 * w3)
        w1 = p01 * r[0] + p11 * r[1] - (g21 * w2 + g31 * w3)
        return [w0, w1, w2, w3]

    def normalized(r):
        z2 = r[2] - (g20 * r[0] + g21 * r[1])
        z3 = r[3] - (g30 * r[0] + g31 * r[1])
        root0, root2 = lax.rsqrt(a[0][0]), lax.rsqrt(s22)
        l10, l32 = a[1][0] * (root0 * root0), s32 * (root2 * root2)
        return [
            r[0] * root0,
            (r[1] - l10 * r[0]) * lax.rsqrt(a[1][1] - l10 * a[1][0]),
            z2 * root2,
            (z3 - l32 * z2) * lax.rsqrt(s33 - l32 * s32),
        ]

    return solve, normalized


def combined(weights, rows):
    return (weights[0] * rows[0] + weights[1] * rows[1]) + (weights[2] * rows[2] + weights[3] * rows[3])


def inverse_rows(gram, tile_refs):
    vecs = gram.shape[0]
    tile, block = 8, 4
    tiles = vecs // tile
    sub_id = lax.broadcasted_iota(jnp.int32, (tile, vecs), 0)
    lane_id = lax.broadcasted_iota(jnp.int32, (tile, vecs), 1)
    diag = [jnp.where(lane_id == sub_id + t * tile, gram[t * tile : (t + 1) * tile], 0.0) for t in range(tiles)]
    scale = lax.rsqrt(jnp.sum(functools.reduce(jnp.add, diag), axis=0, keepdims=True))
    left, right = [], []
    for t in range(tiles):
        own = lax.rsqrt(jnp.sum(diag[t], axis=1, keepdims=True))
        left.append(gram[t * tile : (t + 1) * tile] * scale * own)
        right.append(jnp.where(lane_id == sub_id + t * tile, jnp.broadcast_to(scale, (tile, vecs)), 0.0))

    def lane(x, k):
        return jnp.broadcast_to(x[:, k : k + 1], (tile, vecs))

    def rows_of(tiles_now):
        for ref, x in zip(tile_refs, tiles_now):
            ref[...] = x
        return [[ref[pl.ds(i, tile, stride=0), :] for i in range(tile)] for ref in tile_refs]

    done = []
    for at in range(tiles):
        k = at * tile
        both_rows = rows_of((left[at], right[at]))
        a = [[lane(both_rows[0][i], k + j) for i in range(j + 1)] for j in range(tile)]
        solve, normalized = four_pivots(a)
        inner = [solve(a[j][:block]) for j in range(block, tile)]
        after = [
            [a[block + j][block + i] - combined(a[block + j], inner[i]) for i in range(j + 1)] for j in range(block)
        ]
        solve_after, normalized_after = four_pivots(after)
        weights = []
        for rows in both_rows:
            first = solve(rows[:block])
            later = [rows[block + j] - combined(a[block + j], first) for j in range(block)]
            second = solve_after(later)
            first = [w - combined([inner[j][i] for j in range(block)], second) for i, w in enumerate(first)]
            weights.append(first + second)
        done += [x[:1] for x in normalized(rows[:block]) + normalized_after(later)]
        for t in range(at + 1, tiles):
            cols = [lane(left[t], k + i) for i in range(tile)]
            for part, w in zip((left, right), weights):
                part[t] = part[t] - (combined(cols[:block], w[:block]) + combined(cols[block:], w[block:]))
    return jnp.concatenate(done, axis=0)


def ortho_kernel(scale, *refs):
    *gram_refs, halves_ref, out_ref, left_ref, right_ref = refs
    gram = functools.reduce(jnp.add, [ref[...] for ref in gram_refs])
    width = gram.shape[1]
    inverse = jnp.concatenate(split(inverse_rows(unpacked(gram), (left_ref, right_ref)) * scale), axis=0)
    both = lax.dot_general(
        halves_ref[...],
        jnp.concatenate([inverse, inverse], axis=1),
        (((1,), (1,)), ((), ())),
        preferred_element_type=f32,
    )
    out_ref[...] = both[:, :width] + both[:, width:]


def call(body, out_shape, flops=0, moved=0, limit=24, **kw):
    return pl.pallas_call(
        body,
        out_shape=out_shape,
        compiler_params=pltpu.CompilerParams(vmem_limit_bytes=limit * 1024 * 1024),
        cost_estimate=pl.CostEstimate(flops=flops, bytes_accessed=moved, transcendentals=0),
        **kw,
    )


def swap(value, even, odd):
    poles, groups = lax.axis_size("pole"), lax.axis_size("sub")
    pairs = []
    for p in range(poles):
        for s in range(groups):
            pole_mask, sub_mask = odd if s % 2 else even
            pairs.append((p * groups + s, (p ^ pole_mask) * groups + (s ^ sub_mask)))
    return lax.ppermute(value, ("pole", "sub"), pairs)


def per_device(start_block, inverses, iface_rows, neighbors, couplings, pole_weights):
    blocks = inverses[0]
    sub_count, block_len = blocks.shape[:2]
    vecs = start_block.shape[1]
    iface_len = iface_rows.shape[2]
    poles, groups = lax.axis_size("pole"), lax.axis_size("sub")
    fields = start_block.reshape(sub_count, block_len, vecs)
    shape = jax.ShapeDtypeStruct
    smem = pl.BlockSpec(memory_space=pltpu.SMEM)
    hbm = pl.BlockSpec(memory_space=pltpu.HBM)
    vmem = pl.BlockSpec(memory_space=pltpu.VMEM)
    block_bytes = sub_count * block_len * block_len * 4
    field_bytes = sub_count * block_len * vecs * 4
    packed = shape((sub_count, iface_len // 2, vecs), f32)
    in_hbm = functools.partial(pltpu.with_memory_space_constraint, memory_space=pltpu.HBM)
    in_vmem = functools.partial(pltpu.with_memory_space_constraint, memory_space=pltpu.VMEM)
    sides = shape((sub_count, iface_len, vecs), f32)
    halves = shape(blocks.shape, bf16)
    first, off_side, off0, inv_high, inv_low = call(
        first_kernel,
        (shape(fields.shape, f32), sides, packed, halves, halves),
        flops=8 * sub_count * block_len * block_len * vecs,
        moved=block_bytes + 3 * field_bytes,
        in_specs=[smem] + [hbm] * 3,
        out_specs=[vmem] * 5,
        scratch_shapes=[
            pltpu.VMEM(blocks.shape, f32),
            pltpu.VMEM(fields.shape, f32),
            pltpu.SMEM(iface_rows.shape, jnp.int32),
            pltpu.SemaphoreType.DMA((sub_count,)),
            pltpu.SemaphoreType.DMA((sub_count,)),
            pltpu.SemaphoreType.DMA,
        ],
        name="first_pass",
    )(pole_weights, *[in_hbm(v) for v in (blocks, fields, iface_rows)])
    first, off_side, inv_high, inv_low = (in_vmem(v) for v in (first, off_side, inv_high, inv_low))
    across = [(s, (s + (1 if s % 2 else -1)) % groups) for s in range(groups)]
    inside = [(s, s ^ 1) for s in range(groups)]
    off_in0 = lax.ppermute(off0, "sub", across)
    cols = shape((sub_count, block_len, 2 * iface_len), bf16)
    pass_half = shape((sub_count, 2, block_len // 4, vecs), f32)
    cols_high, cols_low, pass0, pass1, off1, on0, on1, table = call(
        columns_kernel,
        (cols, cols, pass_half, pass_half, packed, packed, packed, shape((2, sub_count, 8, vecs), jnp.int32)),
        flops=8 * sub_count * block_len * block_len * iface_len,
        moved=2 * block_bytes,
        in_specs=[hbm] + [vmem] * 7,
        out_specs=[vmem] * 8,
        scratch_shapes=[
            pltpu.VMEM(sides.shape, f32),
            pltpu.SMEM(iface_rows.shape, jnp.int32),
            pltpu.SemaphoreType.DMA,
        ],
        name="interface_columns",
    )(in_hbm(iface_rows), inv_high, inv_low, iface_rows, couplings, neighbors.T, first, off_side)
    on_in0 = lax.ppermute(on0, "sub", inside)
    on1, off_in0 = lax.optimization_barrier((on1, off_in0))
    halves = [(off_in0, on_in0), (lax.ppermute(off1, "sub", across), lax.ppermute(on1, "sub", inside))]
    cols_high, cols_low, pass0, pass1 = (in_vmem(v) for v in (cols_high, cols_low, pass0, pass1))

    per_owner = sub_count // poles
    steps = poles.bit_length() - 1
    pending = []
    for arrays, own_pass, (off_in, on_in) in zip((2, 2), (pass0, pass1), halves):
        send, keep = (
            call(
                functools.partial(second_kernel, poles, sent),
                (shape((poles // 2, per_owner * block_len // (2 * arrays), vecs), f32),) * arrays,
                flops=4 * sub_count * block_len * 2 * iface_len * vecs,
                moved=2 * sub_count * block_len * vecs * 4,
                in_specs=[vmem] * 6,
                out_specs=[vmem] * arrays,
                name="second_pass",
            )(table, cols_high, cols_low, own_pass, off_in, on_in)
            for sent in (1, 0)
        )
        pending.append([(a, [b]) for a, b in zip(send, keep)])

    for step in range(steps):
        in_order, turned = (1 << step, 0), (1 << (steps - 1 - step), 0)
        for arrays in pending:
            for way, (send, kept) in enumerate(arrays):
                masks = (in_order, turned) if len(arrays) == 1 else ((in_order, turned)[way],) * 2
                kept = kept + [swap(send, *masks)]
                if kept[0].shape[0] > 1:
                    send = functools.reduce(jnp.add, [v[1::2] for v in kept])
                    kept = [v[0::2] for v in kept]
                arrays[way] = (send, kept)

    summands = [[kept for _, kept in arrays] for arrays in pending]
    sizes = tuple(tuple(len(kept) for kept in arrays) for arrays in summands)
    own_rows = per_owner * block_len
    basis_halves, gram = call(
        functools.partial(gram_kernel, sizes, per_owner),
        (shape((own_rows, 2 * vecs), bf16), shape((vecs // 2 + 8, vecs), f32)),
        flops=4 * own_rows * vecs * vecs,
        moved=5 * own_rows * vecs * 4,
        in_specs=[vmem] * sum(map(sum, sizes)),
        out_specs=[vmem] * 2,
        scratch_shapes=[pltpu.VMEM((own_rows, vecs), f32)],
        name="gram",
    )(*[v for arrays in summands for kept in arrays for v in kept])

    stages = [[(0, 1)], [(r, 0) for r in range(1, poles)]]
    stages += [[(0, 1 << bit)] for bit in range(1, groups.bit_length() - 1)]
    grams = [gram]
    for masks in stages:
        total = functools.reduce(jnp.add, grams)
        grams = [total] + [swap(total, m, m) for m in masks]

    total_rows = sub_count * block_len * groups
    return call(
        functools.partial(ortho_kernel, math.sqrt(total_rows)),
        shape((own_rows, vecs), f32),
        flops=6 * own_rows * vecs * vecs,
        moved=2 * own_rows * vecs * 4,
        in_specs=[vmem] * (len(grams) + 1),
        out_specs=vmem,
        scratch_shapes=[pltpu.VMEM((8, vecs), f32)] * 2,
        name="ortho",
    )(*grams, basis_halves)


def solution(mesh):
    placed = (
        P("sub", None),
        P("pole", "sub", None, None),
        P("sub", None, None),
        P("sub", None),
        P("sub", None, None),
        P("pole"),
    )
    return jax.shard_map(
        per_device, mesh=mesh, in_specs=placed, out_specs=P(("sub", "pole"), None), check_vma=False
    )
```

```python
import functools
import math

import jax
import jax.numpy as jnp
from jax import lax
from jax.experimental import pallas as pl
from jax.experimental.pallas import tpu as pltpu
from jax.sharding import PartitionSpec as P

f32 = jnp.float32
bf16 = jnp.bfloat16


def split(x):
    high = x.astype(bf16)
    low = (x - high.astype(f32)).astype(bf16)
    return high, low


def mm(a, b):
    return jnp.dot(a, b, preferred_element_type=f32)


def split_dot(a, b):
    width = b.shape[1]
    both = jnp.concatenate(split(b), axis=1)
    both = mm(a[0], both) + mm(a[1], both)
    return both[:, :width] + both[:, width:]


def turn(x):
    return pltpu.roll(x, x.shape[1] // 2, 1)


def left_lanes(x):
    return lax.broadcasted_iota(jnp.int32, x.shape, 1) < x.shape[1] // 2


def pack(top, bottom, half):
    if half == 0:
        return jnp.where(left_lanes(top), top, turn(bottom))
    return jnp.where(left_lanes(top), turn(top), bottom)


def sub_parity():
    return lax.rem(lax.axis_index("sub"), 2)


def pack_side(side_ref, s, half):
    rows = side_ref.shape[1] // 2
    return pack(side_ref[s, :rows, :], side_ref[s, rows:, :], half)


def gather_side(s, side, pass_ref, rows, side_ref, out_ref):
    for k in range(rows.shape[2]):
        side_ref[s, k : k + 1, :] = pass_ref[s, pl.ds(rows[s, side, k], 1), :]
    out_ref[s] = pack_side(side_ref, s, 0)


def first_kernel(inv_hbm, field_hbm, rows_hbm, pass_ref, side_ref, off_ref, inv_high_ref, inv_low_ref,
                 inv_buf, field_buf, rows, inv_sems, field_sems, rows_sem):
    count = field_buf.shape[0]
    rows_copy = pltpu.make_async_copy(rows_hbm, rows, rows_sem)
    rows_copy.start()

    def copies(s):
        return (
            pltpu.make_async_copy(field_hbm.at[s], field_buf.at[s], field_sems.at[s]),
            pltpu.make_async_copy(inv_hbm.at[s], inv_buf.at[s], inv_sems.at[s]),
        )

    for s in range(count):
        for copy in copies(s):
            copy.start()
    rows_copy.wait()
    parity = sub_parity()

    def one_sub(s, carry):
        for copy in copies(s):
            copy.wait()
        parts = split(inv_buf[s])
        result = split_dot(parts, field_buf[s])
        gather_side(jnp.maximum(s - 1, 0), parity, pass_ref, rows, side_ref, off_ref)
        inv_high_ref[s], inv_low_ref[s] = parts
        pass_ref[s] = result
        return carry

    lax.fori_loop(0, count, one_sub, 0)
    gather_side(count - 1, parity, pass_ref, rows, side_ref, off_ref)


def columns_kernel(rows_hbm, weight_ref, inv_high_ref, inv_low_ref, rows_ref, coup_ref, near_ref, pass_ref, off_side_ref,
                   high_cols_ref, low_cols_ref, off_ref, on0_ref, on1_ref, table_ref, wide_ref,
                   on_side_ref, rows, rows_sem):
    count, block_len = inv_high_ref.shape[:2]
    iface_len = rows_ref.shape[2]

    rows_copy = pltpu.make_async_copy(rows_hbm, rows, rows_sem)
    rows_copy.start()
    parity = sub_parity()
    for spot, side in enumerate((parity, 1 - parity)):
        near = lax.rem(near_ref[pl.ds(side, 1), :], count)
        for s in range(count):
            table_ref[spot, s] = jnp.broadcast_to(near[:, s : s + 1], table_ref.shape[2:])
    weight = weight_ref[0]
    wide_ref[...] = jnp.full(wide_ref.shape, weight, f32)
    place = lax.broadcasted_iota(jnp.int32, (block_len, 2 * iface_len), 0)
    rows_copy.wait()

    def one_sub(s, carry):
        at, coup = (
            jnp.concatenate([ref[s, pl.ds(side, 1), :] for side in (parity, 1 - parity)], axis=1)
            for ref in (rows_ref, coup_ref)
        )
        pick = (at == place).astype(f32).astype(bf16)
        high, low = split((mm(inv_high_ref[s], pick) + mm(inv_low_ref[s], pick)) * (coup * weight))
        gather_side(s, 1 - parity, pass_ref, rows, on_side_ref, on0_ref)
        on1_ref[s] = pack_side(on_side_ref, s, 1)
        off_ref[s] = pack_side(off_side_ref, s, 1)
        high_cols_ref[s] = high
        low_cols_ref[s] = low
        return carry

    lax.fori_loop(0, count, one_sub, 0)


def second_kernel(poles, half, sent, table_ref, wide_ref, high_ref, low_ref, pass_ref, off_ref, on_ref, *out_refs):
    count, block_len, _ = pass_ref.shape
    ways, quarter = 2, block_len // 4
    per_owner = count // poles
    steps = poles.bit_length() - 1
    me, parity = lax.axis_index("pole"), sub_parity()
    split_ways = len(out_refs) == ways
    for r in range(sent, poles, 2):
        turned = sum(1 << (steps - 1 - step) for step in range(steps) if r >> step & 1)
        if split_ways:
            owners = [(me ^ r, [0]), (me ^ turned, [1])]
        else:
            owners = [(me ^ jnp.where(parity == 0, r, turned), [0, 1])]
        for c in range(per_owner):
            for owner, own_ways in owners:
                sub = owner * per_owner + c
                terms = []
                for spot, ref in enumerate((off_ref, on_ref)):
                    near = jnp.concatenate([table_ref[spot, sub]] * (ref.shape[1] // 8), axis=0)
                    side = ref[0]
                    for at in range(1, count):
                        side = jnp.where(near == at, ref[at], side)
                    turned_side = turn(side)
                    terms += [
                        jnp.where(left_lanes(side), side, turned_side),
                        jnp.where(left_lanes(side), turned_side, side),
                    ]
                terms = jnp.concatenate(terms, axis=0)
                high = terms.astype(bf16).astype(f32)
                both = jnp.where(left_lanes(terms), high, terms - high).astype(bf16)
                start, stop = 2 * own_ways[0] * quarter, 2 * (own_ways[-1] + 1) * quarter
                out = mm(high_ref[sub, start:stop, :], both) + mm(low_ref[sub, start:stop, :], both)
                out = out + turn(out)
                for spot, way in enumerate(own_ways):
                    at = 2 * spot * quarter
                    top, bottom = out[at : at + quarter], out[at + quarter : at + 2 * quarter]
                    at = 2 * way * quarter
                    own = pack(pass_ref[sub, at : at + quarter, :], pass_ref[sub, at + quarter : at + 2 * quarter, :], half)
                    to = (c * len(own_ways) + spot) * quarter
                    out_refs[way if split_ways else 0][r // 2, to : to + quarter, :] = (
                        jnp.where(left_lanes(top), top, bottom) + own * wide_ref[0:1, :]
                    )


def gram_kernel(halves, per_owner, *refs):
    count = sum(size for sizes in halves for size in sizes)
    ins, (halves_ref, gram_ref, out_ref) = refs[:count], refs[count:]
    parts = []
    at = 0
    for sizes in halves:
        parts.append([])
        for size in sizes:
            parts[-1].append(functools.reduce(jnp.add, [ref[0] for ref in ins[at : at + size]]))
            at += size
    quarter = out_ref.shape[0] // (4 * per_owner)

    def piece(arrays, c, way):
        spot = c if len(arrays) == 2 else 2 * c + way
        return arrays[way % len(arrays)][spot * quarter : (spot + 1) * quarter]

    for way in range(2):
        for c in range(per_owner):
            first, second = (piece(arrays, c, way) for arrays in parts)
            at = (4 * c + 2 * way) * quarter
            out_ref[at : at + quarter, :] = jnp.where(left_lanes(first), first, turn(second))
            out_ref[at + quarter : at + 2 * quarter, :] = jnp.where(left_lanes(first), turn(first), second)
    high, low = split(out_ref[...])
    width = out_ref.shape[1]
    halves = jnp.concatenate([high, low], axis=1)
    halves_ref[...] = halves
    both = lax.dot_general(high, halves, (((0,), (0,)), ((), ())), preferred_element_type=f32)
    cross = both[:, width:]
    gram = both[:, :width] + (cross + cross.T)
    half = width // 2
    row = lax.broadcasted_iota(jnp.int32, (half, width), 0)
    col = lax.broadcasted_iota(jnp.int32, (half, width), 1)
    gram_ref[:half, :] = jnp.where(row > col - half, jnp.where(col < half, gram[half:], turn(gram[:half])), gram[half:])
    diag = jnp.sum(jnp.where(row == col, gram[:half], 0.0), axis=0, keepdims=True)
    gram_ref[half:, :] = jnp.broadcast_to(diag, (gram_ref.shape[0] - half, width))


def unpacked(gram):
    width = gram.shape[1]
    half = width // 2
    row = lax.broadcasted_iota(jnp.int32, (half, width), 0)
    col = lax.broadcasted_iota(jnp.int32, (half, width), 1)
    top = gram[:half]
    diag = jnp.broadcast_to(gram[half : half + 1], top.shape)
    first = jnp.where(row > col, turn(top), jnp.where(row == col, 0.5 * diag, 0.0))
    last = jnp.where(col < half, top, jnp.where(col - half > row, top, jnp.where(col - half == row, 0.5 * top, 0.0)))
    lower = jnp.concatenate([first, last], axis=0)
    return lower + lower.T


def four_pivots(a):
    det = a[0][0] * a[1][1] - a[1][0] * a[1][0]
    inv = 1.0 / det
    p00, p01, p11 = a[1][1] * inv, -a[1][0] * inv, a[0][0] * inv
    g20, g21 = a[2][0] * p00 + a[2][1] * p01, a[2][0] * p01 + a[2][1] * p11
    g30, g31 = a[3][0] * p00 + a[3][1] * p01, a[3][0] * p01 + a[3][1] * p11
    s22 = a[2][2] - (g20 * a[2][0] + g21 * a[2][1])
    s32 = a[3][2] - (g30 * a[2][0] + g31 * a[2][1])
    s33 = a[3][3] - (g30 * a[3][0] + g31 * a[3][1])
    inv = 1.0 / (s22 * s33 - s32 * s32)
    q00, q01, q11 = s33 * inv, -s32 * inv, s22 * inv

    def solve(r):
        z2 = r[2] - (g20 * r[0] + g21 * r[1])
        z3 = r[3] - (g30 * r[0] + g31 * r[1])
        w2, w3 = q00 * z2 + q01 * z3, q01 * z2 + q11 * z3
        w0 = p00 * r[0] + p01 * r[1] - (g20 * w2 + g30 * w3)
        w1 = p01 * r[0] + p11 * r[1] - (g21 * w2 + g31 * w3)
        return [w0, w1, w2, w3]

    def normalized(r):
        z2 = r[2] - (g20 * r[0] + g21 * r[1])
        z3 = r[3] - (g30 * r[0] + g31 * r[1])
        root0, root2 = lax.rsqrt(a[0][0]), lax.rsqrt(s22)
        l10, l32 = a[1][0] * (root0 * root0), s32 * (root2 * root2)
        return [
            r[0] * root0,
            (r[1] - l10 * r[0]) * lax.rsqrt(a[1][1] - l10 * a[1][0]),
            z2 * root2,
            (z3 - l32 * z2) * lax.rsqrt(s33 - l32 * s32),
        ]

    return solve, normalized


def combined(weights, rows):
    return (weights[0] * rows[0] + weights[1] * rows[1]) + (weights[2] * rows[2] + weights[3] * rows[3])


def inverse_rows(gram, tile_refs):
    vecs = gram.shape[0]
    tile, block = 8, 4
    tiles = vecs // tile
    sub_id = lax.broadcasted_iota(jnp.int32, (tile, vecs), 0)
    lane_id = lax.broadcasted_iota(jnp.int32, (tile, vecs), 1)
    diag = [jnp.where(lane_id == sub_id + t * tile, gram[t * tile : (t + 1) * tile], 0.0) for t in range(tiles)]
    scale = lax.rsqrt(jnp.sum(functools.reduce(jnp.add, diag), axis=0, keepdims=True))
    left, right = [], []
    for t in range(tiles):
        own = lax.rsqrt(jnp.sum(diag[t], axis=1, keepdims=True))
        left.append(gram[t * tile : (t + 1) * tile] * scale * own)
        right.append(jnp.where(lane_id == sub_id + t * tile, jnp.broadcast_to(scale, (tile, vecs)), 0.0))

    def lane(x, k):
        return jnp.broadcast_to(x[:, k : k + 1], (tile, vecs))

    def rows_of(tiles_now):
        for ref, x in zip(tile_refs, tiles_now):
            ref[...] = x
        return [[ref[pl.ds(i, tile, stride=0), :] for i in range(tile)] for ref in tile_refs]

    done = []
    for at in range(tiles):
        k = at * tile
        both_rows = rows_of((left[at], right[at]))
        a = [[lane(both_rows[0][i], k + j) for i in range(j + 1)] for j in range(tile)]
        solve, normalized = four_pivots(a)
        inner = [solve(a[j][:block]) for j in range(block, tile)]
        after = [
            [a[block + j][block + i] - combined(a[block + j], inner[i]) for i in range(j + 1)] for j in range(block)
        ]
        solve_after, normalized_after = four_pivots(after)
        weights = []
        for rows in both_rows:
            first = solve(rows[:block])
            later = [rows[block + j] - combined(a[block + j], first) for j in range(block)]
            second = solve_after(later)
            first = [w - combined([inner[j][i] for j in range(block)], second) for i, w in enumerate(first)]
            weights.append(first + second)
        done += [x[:1] for x in normalized(rows[:block]) + normalized_after(later)]
        for t in range(at + 1, tiles):
            cols = [lane(left[t], k + i) for i in range(tile)]
            for part, w in zip((left, right), weights):
                part[t] = part[t] - (combined(cols[:block], w[:block]) + combined(cols[block:], w[block:]))
    return jnp.concatenate(done, axis=0)


def ortho_kernel(scale, *refs):
    *gram_refs, halves_ref, out_ref, left_ref, right_ref = refs
    gram = functools.reduce(jnp.add, [ref[...] for ref in gram_refs])
    width = gram.shape[1]
    inverse = jnp.concatenate(split(inverse_rows(unpacked(gram), (left_ref, right_ref)) * scale), axis=0)
    both = lax.dot_general(
        halves_ref[...],
        jnp.concatenate([inverse, inverse], axis=1),
        (((1,), (1,)), ((), ())),
        preferred_element_type=f32,
    )
    out_ref[...] = both[:, :width] + both[:, width:]


def call(body, out_shape, flops=0, moved=0, limit=24, **kw):
    return pl.pallas_call(
        body,
        out_shape=out_shape,
        compiler_params=pltpu.CompilerParams(vmem_limit_bytes=limit * 1024 * 1024),
        cost_estimate=pl.CostEstimate(flops=flops, bytes_accessed=moved, transcendentals=0),
        **kw,
    )


def swap(value, even, odd):
    poles, groups = lax.axis_size("pole"), lax.axis_size("sub")
    pairs = []
    for p in range(poles):
        for s in range(groups):
            pole_mask, sub_mask = odd if s % 2 else even
            pairs.append((p * groups + s, (p ^ pole_mask) * groups + (s ^ sub_mask)))
    return lax.ppermute(value, ("pole", "sub"), pairs)


def per_device(start_block, inverses, iface_rows, neighbors, couplings, pole_weights):
    blocks = inverses[0]
    sub_count, block_len = blocks.shape[:2]
    vecs = start_block.shape[1]
    iface_len = iface_rows.shape[2]
    poles, groups = lax.axis_size("pole"), lax.axis_size("sub")
    fields = start_block.reshape(sub_count, block_len, vecs)
    shape = jax.ShapeDtypeStruct
    hbm = pl.BlockSpec(memory_space=pltpu.HBM)
    vmem = pl.BlockSpec(memory_space=pltpu.VMEM)
    block_bytes = sub_count * block_len * block_len * 4
    field_bytes = sub_count * block_len * vecs * 4
    packed = shape((sub_count, iface_len // 2, vecs), f32)
    in_hbm = functools.partial(pltpu.with_memory_space_constraint, memory_space=pltpu.HBM)
    in_vmem = functools.partial(pltpu.with_memory_space_constraint, memory_space=pltpu.VMEM)
    sides = shape((sub_count, iface_len, vecs), f32)
    halves = shape(blocks.shape, bf16)
    first, off_side, off0, inv_high, inv_low = call(
        first_kernel,
        (shape(fields.shape, f32), sides, packed, halves, halves),
        flops=8 * sub_count * block_len * block_len * vecs,
        moved=block_bytes + 3 * field_bytes,
        in_specs=[hbm] * 3,
        out_specs=[vmem] * 5,
        scratch_shapes=[
            pltpu.VMEM(blocks.shape, f32),
            pltpu.VMEM(fields.shape, f32),
            pltpu.SMEM(iface_rows.shape, jnp.int32),
            pltpu.SemaphoreType.DMA((sub_count,)),
            pltpu.SemaphoreType.DMA((sub_count,)),
            pltpu.SemaphoreType.DMA,
        ],
        name="first_pass",
    )(*[in_hbm(v) for v in (blocks, fields, iface_rows)])
    first, off_side, inv_high, inv_low = (in_vmem(v) for v in (first, off_side, inv_high, inv_low))
    across = [(s, (s + (1 if s % 2 else -1)) % groups) for s in range(groups)]
    inside = [(s, s ^ 1) for s in range(groups)]
    off_in0 = lax.ppermute(off0, "sub", across)
    cols = shape((sub_count, block_len, 2 * iface_len), bf16)
    cols_high, cols_low, off1, on0, on1, table, wide = call(
        columns_kernel,
        (cols, cols, packed, packed, packed, shape((2, sub_count, 8, vecs), jnp.int32), shape((8, vecs), f32)),
        flops=8 * sub_count * block_len * block_len * iface_len,
        moved=2 * block_bytes,
        in_specs=[hbm, pl.BlockSpec(memory_space=pltpu.SMEM)] + [vmem] * 7,
        out_specs=[vmem] * 7,
        scratch_shapes=[
            pltpu.VMEM(sides.shape, f32),
            pltpu.SMEM(iface_rows.shape, jnp.int32),
            pltpu.SemaphoreType.DMA,
        ],
        name="interface_columns",
    )(in_hbm(iface_rows), pole_weights, inv_high, inv_low, iface_rows, couplings, neighbors.T, first, off_side)
    on_in0 = lax.ppermute(on0, "sub", inside)
    on1, off_in0 = lax.optimization_barrier((on1, off_in0))
    halves = [(off_in0, on_in0), (lax.ppermute(off1, "sub", across), lax.ppermute(on1, "sub", inside))]
    cols_high, cols_low = in_vmem(cols_high), in_vmem(cols_low)

    per_owner = sub_count // poles
    steps = poles.bit_length() - 1
    pending = []
    for half, (arrays, (off_in, on_in)) in enumerate(zip((2, 2), halves)):
        send, keep = (
            call(
                functools.partial(second_kernel, poles, half, sent),
                (shape((poles // 2, per_owner * block_len // (2 * arrays), vecs), f32),) * arrays,
                flops=4 * sub_count * block_len * 2 * iface_len * vecs,
                moved=2 * sub_count * block_len * vecs * 4,
                in_specs=[vmem] * 7,
                out_specs=[vmem] * arrays,
                name="second_pass",
            )(table, wide, cols_high, cols_low, first, off_in, on_in)
            for sent in (1, 0)
        )
        pending.append([(a, [b]) for a, b in zip(send, keep)])

    for step in range(steps):
        in_order, turned = (1 << step, 0), (1 << (steps - 1 - step), 0)
        for arrays in pending:
            for way, (send, kept) in enumerate(arrays):
                masks = (in_order, turned) if len(arrays) == 1 else ((in_order, turned)[way],) * 2
                kept = kept + [swap(send, *masks)]
                if kept[0].shape[0] > 1:
                    send = functools.reduce(jnp.add, [v[1::2] for v in kept])
                    kept = [v[0::2] for v in kept]
                arrays[way] = (send, kept)

    summands = [[kept for _, kept in arrays] for arrays in pending]
    sizes = tuple(tuple(len(kept) for kept in arrays) for arrays in summands)
    own_rows = per_owner * block_len
    basis_halves, gram = call(
        functools.partial(gram_kernel, sizes, per_owner),
        (shape((own_rows, 2 * vecs), bf16), shape((vecs // 2 + 8, vecs), f32)),
        flops=4 * own_rows * vecs * vecs,
        moved=5 * own_rows * vecs * 4,
        in_specs=[vmem] * sum(map(sum, sizes)),
        out_specs=[vmem] * 2,
        scratch_shapes=[pltpu.VMEM((own_rows, vecs), f32)],
        name="gram",
    )(*[v for arrays in summands for kept in arrays for v in kept])

    stages = [[(0, 1)], [(r, 0) for r in range(1, poles)]]
    base = 2
    while base < groups:
        radix = min(4, groups // base)
        stages.append([(0, base * r) for r in range(1, radix)])
        base *= radix
    grams = [gram]
    for masks in stages:
        total = functools.reduce(jnp.add, grams)
        grams = [total] + [swap(total, m, m) for m in masks]

    total_rows = sub_count * block_len * groups
    return call(
        functools.partial(ortho_kernel, math.sqrt(total_rows)),
        shape((own_rows, vecs), f32),
        flops=6 * own_rows * vecs * vecs,
        moved=2 * own_rows * vecs * 4,
        in_specs=[vmem] * (len(grams) + 1),
        out_specs=vmem,
        scratch_shapes=[pltpu.VMEM((8, vecs), f32)] * 2,
        name="ortho",
    )(*grams, basis_halves)


def solution(mesh):
    placed = (
        P("sub", None),
        P("pole", "sub", None, None),
        P("sub", None, None),
        P("sub", None),
        P("sub", None, None),
        P("pole"),
    )
    return jax.shard_map(
        per_device, mesh=mesh, in_specs=placed, out_specs=P(("sub", "pole"), None), check_vma=False
    )
```

```python
import functools
import math

import jax
import jax.numpy as jnp
from jax import lax
from jax.experimental import pallas as pl
from jax.experimental.pallas import tpu as pltpu
from jax.sharding import PartitionSpec as P

f32 = jnp.float32
bf16 = jnp.bfloat16


def split(x):
    high = x.astype(bf16)
    low = (x - high.astype(f32)).astype(bf16)
    return high, low


def mm(a, b):
    return jnp.dot(a, b, preferred_element_type=f32)


def split_dot(a, b):
    width = b.shape[1]
    both = jnp.concatenate(split(b), axis=1)
    both = mm(a[0], both) + mm(a[1], both)
    return both[:, :width] + both[:, width:]


def turn(x):
    return pltpu.roll(x, x.shape[1] // 2, 1)


def left_lanes(x):
    return lax.broadcasted_iota(jnp.int32, x.shape, 1) < x.shape[1] // 2


def pack(top, bottom, half):
    if half == 0:
        return jnp.where(left_lanes(top), top, turn(bottom))
    return jnp.where(left_lanes(top), turn(top), bottom)


def sub_parity():
    return lax.rem(lax.axis_index("sub"), 2)


def pack_side(side_ref, s, half):
    rows = side_ref.shape[1] // 2
    return pack(side_ref[s, :rows, :], side_ref[s, rows:, :], half)


def gather_side(s, side, pass_ref, rows, side_ref, out_ref):
    for k in range(rows.shape[2]):
        side_ref[s, k : k + 1, :] = pass_ref[s, pl.ds(rows[s, side, k], 1), :]
    out_ref[s] = pack_side(side_ref, s, 0)


def first_kernel(inv_hbm, field_hbm, rows_hbm, pass_ref, side_ref, off_ref, inv_high_ref, inv_low_ref,
                 inv_buf, field_buf, rows, inv_sems, field_sems, rows_sem):
    count = field_buf.shape[0]
    rows_copy = pltpu.make_async_copy(rows_hbm, rows, rows_sem)
    rows_copy.start()

    def copies(s):
        return (
            pltpu.make_async_copy(field_hbm.at[s], field_buf.at[s], field_sems.at[s]),
            pltpu.make_async_copy(inv_hbm.at[s], inv_buf.at[s], inv_sems.at[s]),
        )

    for s in range(count):
        for copy in copies(s):
            copy.start()
    rows_copy.wait()
    parity = sub_parity()

    def one_sub(s, carry):
        for copy in copies(s):
            copy.wait()
        parts = split(inv_buf[s])
        result = split_dot(parts, field_buf[s])
        gather_side(jnp.maximum(s - 1, 0), parity, pass_ref, rows, side_ref, off_ref)
        inv_high_ref[s], inv_low_ref[s] = parts
        pass_ref[s] = result
        return carry

    lax.fori_loop(0, count, one_sub, 0)
    gather_side(count - 1, parity, pass_ref, rows, side_ref, off_ref)


def columns_kernel(rows_hbm, inv_high_ref, inv_low_ref, rows_ref, coup_ref, near_ref, pass_ref, off_side_ref,
                   high_cols_ref, low_cols_ref, off_ref, on0_ref, on1_ref, table_ref,
                   on_side_ref, rows, rows_sem):
    count, block_len = inv_high_ref.shape[:2]
    iface_len = rows_ref.shape[2]

    rows_copy = pltpu.make_async_copy(rows_hbm, rows, rows_sem)
    rows_copy.start()
    parity = sub_parity()
    for spot, side in enumerate((parity, 1 - parity)):
        near = lax.rem(near_ref[pl.ds(side, 1), :], count)
        for s in range(count):
            table_ref[spot, s] = jnp.broadcast_to(near[:, s : s + 1], table_ref.shape[2:])
    place = lax.broadcasted_iota(jnp.int32, (block_len, 2 * iface_len), 0)
    rows_copy.wait()

    def one_sub(s, carry):
        at, coup = (
            jnp.concatenate([ref[s, pl.ds(side, 1), :] for side in (parity, 1 - parity)], axis=1)
            for ref in (rows_ref, coup_ref)
        )
        pick = (at == place).astype(f32).astype(bf16)
        high, low = split((mm(inv_high_ref[s], pick) + mm(inv_low_ref[s], pick)) * coup)
        gather_side(s, 1 - parity, pass_ref, rows, on_side_ref, on0_ref)
        on1_ref[s] = pack_side(on_side_ref, s, 1)
        off_ref[s] = pack_side(off_side_ref, s, 1)
        high_cols_ref[s] = high
        low_cols_ref[s] = low
        return carry

    lax.fori_loop(0, count, one_sub, 0)


def second_kernel(poles, half, sent, weight_ref, table_ref, high_ref, low_ref, pass_ref, off_ref, on_ref, *out_refs):
    count, block_len, _ = pass_ref.shape
    ways, quarter = 2, block_len // 4
    per_owner = count // poles
    steps = poles.bit_length() - 1
    me, parity = lax.axis_index("pole"), sub_parity()
    split_ways = len(out_refs) == ways
    for r in range(sent, poles, 2):
        turned = sum(1 << (steps - 1 - step) for step in range(steps) if r >> step & 1)
        if split_ways:
            owners = [(me ^ r, [0]), (me ^ turned, [1])]
        else:
            owners = [(me ^ jnp.where(parity == 0, r, turned), [0, 1])]
        for c in range(per_owner):
            for owner, own_ways in owners:
                sub = owner * per_owner + c
                terms = []
                for spot, ref in enumerate((off_ref, on_ref)):
                    near = jnp.concatenate([table_ref[spot, sub]] * (ref.shape[1] // 8), axis=0)
                    side = ref[0]
                    for at in range(1, count):
                        side = jnp.where(near == at, ref[at], side)
                    turned_side = turn(side)
                    terms += [
                        jnp.where(left_lanes(side), side, turned_side),
                        jnp.where(left_lanes(side), turned_side, side),
                    ]
                terms = jnp.concatenate(terms, axis=0)
                high = terms.astype(bf16).astype(f32)
                both = jnp.where(left_lanes(terms), high, terms - high).astype(bf16)
                start, stop = 2 * own_ways[0] * quarter, 2 * (own_ways[-1] + 1) * quarter
                out = mm(high_ref[sub, start:stop, :], both) + mm(low_ref[sub, start:stop, :], both)
                out = out + turn(out)
                for spot, way in enumerate(own_ways):
                    at = 2 * spot * quarter
                    top, bottom = out[at : at + quarter], out[at + quarter : at + 2 * quarter]
                    at = 2 * way * quarter
                    own = pack(pass_ref[sub, at : at + quarter, :], pass_ref[sub, at + quarter : at + 2 * quarter, :], half)
                    to = (c * len(own_ways) + spot) * quarter
                    out_refs[way if split_ways else 0][r // 2, to : to + quarter, :] = weight_ref[0] * (
                        jnp.where(left_lanes(top), top, bottom) + own
                    )


def gram_kernel(halves, per_owner, *refs):
    count = sum(size for sizes in halves for size in sizes)
    ins, (halves_ref, gram_ref, out_ref) = refs[:count], refs[count:]
    parts = []
    at = 0
    for sizes in halves:
        parts.append([])
        for size in sizes:
            parts[-1].append(functools.reduce(jnp.add, [ref[0] for ref in ins[at : at + size]]))
            at += size
    quarter = out_ref.shape[0] // (4 * per_owner)

    def piece(arrays, c, way):
        spot = c if len(arrays) == 2 else 2 * c + way
        return arrays[way % len(arrays)][spot * quarter : (spot + 1) * quarter]

    for way in range(2):
        for c in range(per_owner):
            first, second = (piece(arrays, c, way) for arrays in parts)
            at = (4 * c + 2 * way) * quarter
            out_ref[at : at + quarter, :] = jnp.where(left_lanes(first), first, turn(second))
            out_ref[at + quarter : at + 2 * quarter, :] = jnp.where(left_lanes(first), turn(first), second)
    high, low = split(out_ref[...])
    width = out_ref.shape[1]
    halves = jnp.concatenate([high, low], axis=1)
    halves_ref[...] = halves
    both = lax.dot_general(high, halves, (((0,), (0,)), ((), ())), preferred_element_type=f32)
    cross = both[:, width:]
    gram = both[:, :width] + (cross + cross.T)
    half = width // 2
    row = lax.broadcasted_iota(jnp.int32, (half, width), 0)
    col = lax.broadcasted_iota(jnp.int32, (half, width), 1)
    gram_ref[:half, :] = jnp.where(row > col - half, jnp.where(col < half, gram[half:], turn(gram[:half])), gram[half:])
    diag = jnp.sum(jnp.where(row == col, gram[:half], 0.0), axis=0, keepdims=True)
    gram_ref[half:, :] = jnp.broadcast_to(diag, (gram_ref.shape[0] - half, width))


def unpacked(gram):
    width = gram.shape[1]
    half = width // 2
    row = lax.broadcasted_iota(jnp.int32, (half, width), 0)
    col = lax.broadcasted_iota(jnp.int32, (half, width), 1)
    top = gram[:half]
    diag = jnp.broadcast_to(gram[half : half + 1], top.shape)
    first = jnp.where(row > col, turn(top), jnp.where(row == col, 0.5 * diag, 0.0))
    last = jnp.where(col < half, top, jnp.where(col - half > row, top, jnp.where(col - half == row, 0.5 * top, 0.0)))
    lower = jnp.concatenate([first, last], axis=0)
    return lower + lower.T


def four_pivots(a):
    det = a[0][0] * a[1][1] - a[1][0] * a[1][0]
    inv = 1.0 / det
    p00, p01, p11 = a[1][1] * inv, -a[1][0] * inv, a[0][0] * inv
    g20, g21 = a[2][0] * p00 + a[2][1] * p01, a[2][0] * p01 + a[2][1] * p11
    g30, g31 = a[3][0] * p00 + a[3][1] * p01, a[3][0] * p01 + a[3][1] * p11
    s22 = a[2][2] - (g20 * a[2][0] + g21 * a[2][1])
    s32 = a[3][2] - (g30 * a[2][0] + g31 * a[2][1])
    s33 = a[3][3] - (g30 * a[3][0] + g31 * a[3][1])
    inv = 1.0 / (s22 * s33 - s32 * s32)
    q00, q01, q11 = s33 * inv, -s32 * inv, s22 * inv

    def solve(r):
        z2 = r[2] - (g20 * r[0] + g21 * r[1])
        z3 = r[3] - (g30 * r[0] + g31 * r[1])
        w2, w3 = q00 * z2 + q01 * z3, q01 * z2 + q11 * z3
        w0 = p00 * r[0] + p01 * r[1] - (g20 * w2 + g30 * w3)
        w1 = p01 * r[0] + p11 * r[1] - (g21 * w2 + g31 * w3)
        return [w0, w1, w2, w3]

    def normalized(r):
        z2 = r[2] - (g20 * r[0] + g21 * r[1])
        z3 = r[3] - (g30 * r[0] + g31 * r[1])
        root0, root2 = lax.rsqrt(a[0][0]), lax.rsqrt(s22)
        l10, l32 = a[1][0] * (root0 * root0), s32 * (root2 * root2)
        return [
            r[0] * root0,
            (r[1] - l10 * r[0]) * lax.rsqrt(a[1][1] - l10 * a[1][0]),
            z2 * root2,
            (z3 - l32 * z2) * lax.rsqrt(s33 - l32 * s32),
        ]

    return solve, normalized


def combined(weights, rows):
    return (weights[0] * rows[0] + weights[1] * rows[1]) + (weights[2] * rows[2] + weights[3] * rows[3])


def inverse_rows(gram, tile_refs):
    vecs = gram.shape[0]
    tile, block = 8, 4
    tiles = vecs // tile
    sub_id = lax.broadcasted_iota(jnp.int32, (tile, vecs), 0)
    lane_id = lax.broadcasted_iota(jnp.int32, (tile, vecs), 1)
    diag = [jnp.where(lane_id == sub_id + t * tile, gram[t * tile : (t + 1) * tile], 0.0) for t in range(tiles)]
    scale = lax.rsqrt(jnp.sum(functools.reduce(jnp.add, diag), axis=0, keepdims=True))
    left, right = [], []
    for t in range(tiles):
        own = lax.rsqrt(jnp.sum(diag[t], axis=1, keepdims=True))
        left.append(gram[t * tile : (t + 1) * tile] * scale * own)
        right.append(jnp.where(lane_id == sub_id + t * tile, jnp.broadcast_to(scale, (tile, vecs)), 0.0))

    def lane(x, k):
        return jnp.broadcast_to(x[:, k : k + 1], (tile, vecs))

    def rows_of(tiles_now):
        for ref, x in zip(tile_refs, tiles_now):
            ref[...] = x
        return [[ref[pl.ds(i, tile, stride=0), :] for i in range(tile)] for ref in tile_refs]

    done = []
    for at in range(tiles):
        k = at * tile
        both_rows = rows_of((left[at], right[at]))
        a = [[lane(both_rows[0][i], k + j) for i in range(j + 1)] for j in range(tile)]
        solve, normalized = four_pivots(a)
        inner = [solve(a[j][:block]) for j in range(block, tile)]
        after = [
            [a[block + j][block + i] - combined(a[block + j], inner[i]) for i in range(j + 1)] for j in range(block)
        ]
        solve_after, normalized_after = four_pivots(after)
        weights = []
        for rows in both_rows:
            first = solve(rows[:block])
            later = [rows[block + j] - combined(a[block + j], first) for j in range(block)]
            second = solve_after(later)
            first = [w - combined([inner[j][i] for j in range(block)], second) for i, w in enumerate(first)]
            weights.append(first + second)
        done += [x[:1] for x in normalized(rows[:block]) + normalized_after(later)]
        for t in range(at + 1, tiles):
            cols = [lane(left[t], k + i) for i in range(tile)]
            for part, w in zip((left, right), weights):
                part[t] = part[t] - (combined(cols[:block], w[:block]) + combined(cols[block:], w[block:]))
    return jnp.concatenate(done, axis=0)


def ortho_kernel(scale, *refs):
    *gram_refs, halves_ref, out_ref, left_ref, right_ref = refs
    gram = functools.reduce(jnp.add, [ref[...] for ref in gram_refs])
    width = gram.shape[1]
    inverse = jnp.concatenate(split(inverse_rows(unpacked(gram), (left_ref, right_ref)) * scale), axis=0)
    both = lax.dot_general(
        halves_ref[...],
        jnp.concatenate([inverse, inverse], axis=1),
        (((1,), (1,)), ((), ())),
        preferred_element_type=f32,
    )
    out_ref[...] = both[:, :width] + both[:, width:]


def call(body, out_shape, flops=0, moved=0, limit=24, **kw):
    return pl.pallas_call(
        body,
        out_shape=out_shape,
        compiler_params=pltpu.CompilerParams(vmem_limit_bytes=limit * 1024 * 1024),
        cost_estimate=pl.CostEstimate(flops=flops, bytes_accessed=moved, transcendentals=0),
        **kw,
    )


def swap(value, even, odd):
    poles, groups = lax.axis_size("pole"), lax.axis_size("sub")
    pairs = []
    for p in range(poles):
        for s in range(groups):
            pole_mask, sub_mask = odd if s % 2 else even
            pairs.append((p * groups + s, (p ^ pole_mask) * groups + (s ^ sub_mask)))
    return lax.ppermute(value, ("pole", "sub"), pairs)


def per_device(start_block, inverses, iface_rows, neighbors, couplings, pole_weights):
    blocks = inverses[0]
    sub_count, block_len = blocks.shape[:2]
    vecs = start_block.shape[1]
    iface_len = iface_rows.shape[2]
    poles, groups = lax.axis_size("pole"), lax.axis_size("sub")
    fields = start_block.reshape(sub_count, block_len, vecs)
    shape = jax.ShapeDtypeStruct
    hbm = pl.BlockSpec(memory_space=pltpu.HBM)
    vmem = pl.BlockSpec(memory_space=pltpu.VMEM)
    block_bytes = sub_count * block_len * block_len * 4
    field_bytes = sub_count * block_len * vecs * 4
    packed = shape((sub_count, iface_len // 2, vecs), f32)
    in_hbm = functools.partial(pltpu.with_memory_space_constraint, memory_space=pltpu.HBM)
    in_vmem = functools.partial(pltpu.with_memory_space_constraint, memory_space=pltpu.VMEM)
    sides = shape((sub_count, iface_len, vecs), f32)
    halves = shape(blocks.shape, bf16)
    first, off_side, off0, inv_high, inv_low = call(
        first_kernel,
        (shape(fields.shape, f32), sides, packed, halves, halves),
        flops=8 * sub_count * block_len * block_len * vecs,
        moved=block_bytes + 3 * field_bytes,
        in_specs=[hbm] * 3,
        out_specs=[vmem] * 5,
        scratch_shapes=[
            pltpu.VMEM(blocks.shape, f32),
            pltpu.VMEM(fields.shape, f32),
            pltpu.SMEM(iface_rows.shape, jnp.int32),
            pltpu.SemaphoreType.DMA((sub_count,)),
            pltpu.SemaphoreType.DMA((sub_count,)),
            pltpu.SemaphoreType.DMA,
        ],
        name="first_pass",
    )(*[in_hbm(v) for v in (blocks, fields, iface_rows)])
    first, off_side, inv_high, inv_low = (in_vmem(v) for v in (first, off_side, inv_high, inv_low))
    across = [(s, (s + (1 if s % 2 else -1)) % groups) for s in range(groups)]
    inside = [(s, s ^ 1) for s in range(groups)]
    off_in0 = lax.ppermute(off0, "sub", across)
    cols = shape((sub_count, block_len, 2 * iface_len), bf16)
    cols_high, cols_low, off1, on0, on1, table = call(
        columns_kernel,
        (cols, cols, packed, packed, packed, shape((2, sub_count, 8, vecs), jnp.int32)),
        flops=8 * sub_count * block_len * block_len * iface_len,
        moved=2 * block_bytes,
        in_specs=[hbm] + [vmem] * 7,
        out_specs=[vmem] * 6,
        scratch_shapes=[
            pltpu.VMEM(sides.shape, f32),
            pltpu.SMEM(iface_rows.shape, jnp.int32),
            pltpu.SemaphoreType.DMA,
        ],
        name="interface_columns",
    )(in_hbm(iface_rows), inv_high, inv_low, iface_rows, couplings, neighbors.T, first, off_side)
    on_in0 = lax.ppermute(on0, "sub", inside)
    on1, off_in0 = lax.optimization_barrier((on1, off_in0))
    halves = [(off_in0, on_in0), (lax.ppermute(off1, "sub", across), lax.ppermute(on1, "sub", inside))]
    cols_high, cols_low = in_vmem(cols_high), in_vmem(cols_low)

    per_owner = sub_count // poles
    steps = poles.bit_length() - 1
    pending = []
    for half, (arrays, (off_in, on_in)) in enumerate(zip((2, 2), halves)):
        send, keep = (
            call(
                functools.partial(second_kernel, poles, half, sent),
                (shape((poles // 2, per_owner * block_len // (2 * arrays), vecs), f32),) * arrays,
                flops=4 * sub_count * block_len * 2 * iface_len * vecs,
                moved=2 * sub_count * block_len * vecs * 4,
                in_specs=[pl.BlockSpec(memory_space=pltpu.SMEM)] + [vmem] * 6,
                out_specs=[vmem] * arrays,
                name="second_pass",
            )(pole_weights, table, cols_high, cols_low, first, off_in, on_in)
            for sent in (1, 0)
        )
        pending.append([(a, [b]) for a, b in zip(send, keep)])

    for step in range(steps):
        in_order, turned = (1 << step, 0), (1 << (steps - 1 - step), 0)
        for arrays in pending:
            for way, (send, kept) in enumerate(arrays):
                masks = (in_order, turned) if len(arrays) == 1 else ((in_order, turned)[way],) * 2
                kept = kept + [swap(send, *masks)]
                if kept[0].shape[0] > 1:
                    send = functools.reduce(jnp.add, [v[1::2] for v in kept])
                    kept = [v[0::2] for v in kept]
                arrays[way] = (send, kept)

    summands = [[kept for _, kept in arrays] for arrays in pending]
    sizes = tuple(tuple(len(kept) for kept in arrays) for arrays in summands)
    own_rows = per_owner * block_len
    basis_halves, gram = call(
        functools.partial(gram_kernel, sizes, per_owner),
        (shape((own_rows, 2 * vecs), bf16), shape((vecs // 2 + 8, vecs), f32)),
        flops=4 * own_rows * vecs * vecs,
        moved=5 * own_rows * vecs * 4,
        in_specs=[vmem] * sum(map(sum, sizes)),
        out_specs=[vmem] * 2,
        scratch_shapes=[pltpu.VMEM((own_rows, vecs), f32)],
        name="gram",
    )(*[v for arrays in summands for kept in arrays for v in kept])

    stages = [[(0, 1)], [(r, 0) for r in range(1, poles)]]
    base = 2
    while base < groups:
        radix = min(4, groups // base)
        stages.append([(0, base * r) for r in range(1, radix)])
        base *= radix
    grams = [gram]
    for masks in stages:
        total = functools.reduce(jnp.add, grams)
        grams = [total] + [swap(total, m, m) for m in masks]

    total_rows = sub_count * block_len * groups
    return call(
        functools.partial(ortho_kernel, math.sqrt(total_rows)),
        shape((own_rows, vecs), f32),
        flops=6 * own_rows * vecs * vecs,
        moved=2 * own_rows * vecs * 4,
        in_specs=[vmem] * (len(grams) + 1),
        out_specs=vmem,
        scratch_shapes=[pltpu.VMEM((8, vecs), f32)] * 2,
        name="ortho",
    )(*grams, basis_halves)


def solution(mesh):
    placed = (
        P("sub", None),
        P("pole", "sub", None, None),
        P("sub", None, None),
        P("sub", None),
        P("sub", None, None),
        P("pole"),
    )
    return jax.shard_map(
        per_device, mesh=mesh, in_specs=placed, out_specs=P(("sub", "pole"), None), check_vma=False
    )
```
